128 devices in a mesh: row: 16 (over x_lo, y, core), col: 8 (over x_hi, z).
Axes of the slice: x: 4 (x_hi: 2, x_lo: 2; x = x_hi * 2 + x_lo), y: 4, z: 4, core: 2. Of those that a mesh axis runs over, the one named last changes fastest.
Arguments:
- alignment_tensor: bfloat16 [256, 1024, 256], P(None, ('row', 'col')), may hold values from -6 to 6
- amino_exists_flags: int32 [256, 1024], P(None, ('row', 'col')), may hold values 0 or 1
- chain_exists_flags: int32 [256], replicated, may hold values 0 or 1
- chosen_slab_number: int32 [1], replicated, may hold values from 0 to 15
- duo_tensor: bfloat16 [1024, 1024, 128], P('row', 'col'), may hold values from -6 to 6
- duo_offset_matrix: bfloat16 [128, 8], replicated, may hold values from -0.5 to 0.5
- asking_matrix: bfloat16 [256, 256], replicated
- lookup_matrix: bfloat16 [256, 256], replicated
- content_matrix: bfloat16 [256, 256], replicated, may hold values from -0.375 to 0.375
- sigmoid_matrix: bfloat16 [256, 256], replicated, may hold values from -0.375 to 0.375
- final_projection_matrix: bfloat16 [256, 256], replicated, may hold values from -0.375 to 0.375
- first_factor_matrix: bfloat16 [256, 32], replicated, may hold values from -0.375 to 0.375
- second_factor_matrix: bfloat16 [256, 32], replicated, may hold values from -0.375 to 0.375
- product_to_duo_matrix: bfloat16 [1024, 128], replicated, may hold values from -3 to 3
Outputs:
- alignment_reweighted: bfloat16 [256, 1024, 256], P(None, ('row', 'col'))
- product_average: bfloat16 [64, 1024, 128], P(None, ('row', 'col'))
The draws below stay inside these ranges and needn't reach their ends.
All inputs are finite; a program needn't handle non-finite values. No bound on the sum of `amino_exists_flags` on one device may be relied on, other than what follows from the above.
Results may differ from the reference program's by a relative error of at most 0.017.
Values may be sent and summed in bfloat16 or wider, within the bound.
No kernel may reach another device: no remote copies, remote signals or barrier semaphores. Data moves between devices by JAX's collectives and lax.ppermute only.
A program may use at most 128 MiB of HBM per device.

```python
import jax
import jax.numpy as jnp
from jax import lax

ALIGN_FEATURES = 256
DUO_FEATURES = 128
SCORE_GROUPS = 8
GROUP_FEATURES = 32
PROJECTED_WIDTH = 32
AMINO_COUNT = 1024
ALIGN_CHAINS = 256
SLAB = 64
N_ROW = 16


def draw_asking_matrix(key, part):
    key = jax.random.fold_in(key, 1)
    device_portion = jax.random.normal(key, (ALIGN_FEATURES, SCORE_GROUPS * GROUP_FEATURES), jnp.float32)
    return (device_portion / ALIGN_FEATURES ** 0.5).astype(jnp.bfloat16)


def draw_lookup_matrix(key, part):
    key = jax.random.fold_in(key, 2)
    device_portion = jax.random.normal(key, (ALIGN_FEATURES, SCORE_GROUPS * GROUP_FEATURES), jnp.float32)
    return (device_portion / ALIGN_FEATURES ** 0.5).astype(jnp.bfloat16)


def touch_ends(values, key, smallest, top_value):
    shape = values.shape
    index_at = [jax.random.randint(jax.random.fold_in(key, axis), (), 0, shape[axis]) for axis in range(len(shape))]
    values = values.at[tuple(index_at)].set(smallest)
    longest = shape.index(max(shape))
    index_at[longest] = (index_at[longest] + 1) % shape[longest]
    return values.at[tuple(index_at)].set(top_value)


def block_levels(key, extent, split, smallest, largest):
    factor_of, own = 1.0, jax.random.fold_in(key, 6)
    for position, blocks in split:
        steps = jnp.exp(jax.random.uniform(jax.random.fold_in(own, position), (blocks,), jnp.float32, smallest / len(split), largest / len(split)))
        factor_of = factor_of * jnp.repeat(steps, extent[position] // blocks).reshape([-1 if axis == position else 1 for axis in range(len(extent))])
    return factor_of


def gaussian(stream_key, dims, deviation, most, split=(), kind=jnp.bfloat16):
    values = jax.random.normal(stream_key, dims, jnp.float32) * deviation
    if len(split) > 0:
        values = block_levels(stream_key, dims, split, -0.22, 0.18) * values
    return jnp.clip(values, min=-most, max=most).astype(kind)


def setup_inputs(seed: int = 0) -> dict:
    arg_keys = jax.random.split(jax.random.key(seed), 15)
    alignment_tensor = gaussian(arg_keys[0], (ALIGN_CHAINS, AMINO_COUNT, ALIGN_FEATURES), 1.0, 6.0, ((1, 128),))
    amino_exists_flags = touch_ends((jax.random.randint(arg_keys[1], (ALIGN_CHAINS, AMINO_COUNT), 0, 8) < 7).astype(jnp.int32), jax.random.fold_in(arg_keys[1], 1), 0, 1)
    chain_exists_flags = touch_ends((jax.random.randint(arg_keys[2], (ALIGN_CHAINS,), 0, 4) < 3).astype(jnp.int32), jax.random.fold_in(arg_keys[2], 1), 0, 1)
    chosen_slab_number = jax.random.randint(arg_keys[3], (1,), 0, N_ROW).astype(jnp.int32)
    duo_tensor = gaussian(arg_keys[4], (AMINO_COUNT, AMINO_COUNT, DUO_FEATURES), 1.0, 6.0, ((0, 16), (1, 8)))
    duo_offset_matrix = gaussian(arg_keys[5], (DUO_FEATURES, SCORE_GROUPS), DUO_FEATURES ** -0.5, 0.5)
    asking_matrix = draw_asking_matrix(jax.random.fold_in(arg_keys[14], 71), 0)
    lookup_matrix = draw_lookup_matrix(jax.random.fold_in(arg_keys[14], 71), 0)
    content_matrix = gaussian(arg_keys[8], (ALIGN_FEATURES, SCORE_GROUPS * GROUP_FEATURES), ALIGN_FEATURES ** -0.5, 0.375)
    sigmoid_matrix = gaussian(arg_keys[9], (ALIGN_FEATURES, SCORE_GROUPS * GROUP_FEATURES), ALIGN_FEATURES ** -0.5, 0.375)
    final_projection_matrix = gaussian(arg_keys[10], (SCORE_GROUPS * GROUP_FEATURES, ALIGN_FEATURES), (SCORE_GROUPS * GROUP_FEATURES) ** -0.5, 0.375)
    first_factor_matrix = gaussian(arg_keys[11], (ALIGN_FEATURES, PROJECTED_WIDTH), ALIGN_FEATURES ** -0.5, 0.375)
    second_factor_matrix = gaussian(arg_keys[12], (ALIGN_FEATURES, PROJECTED_WIDTH), ALIGN_FEATURES ** -0.5, 0.375)
    product_to_duo_matrix = gaussian(arg_keys[13], (PROJECTED_WIDTH * PROJECTED_WIDTH, DUO_FEATURES), (max(1, PROJECTED_WIDTH * PROJECTED_WIDTH // ALIGN_CHAINS)) ** -0.5, 3.0)
    return {"alignment_tensor": alignment_tensor, "amino_exists_flags": amino_exists_flags, "chain_exists_flags": chain_exists_flags, "chosen_slab_number": chosen_slab_number, "duo_tensor": duo_tensor, "duo_offset_matrix": duo_offset_matrix, "asking_matrix": asking_matrix, "lookup_matrix": lookup_matrix, "content_matrix": content_matrix, "sigmoid_matrix": sigmoid_matrix, "final_projection_matrix": final_projection_matrix, "first_factor_matrix": first_factor_matrix, "second_factor_matrix": second_factor_matrix, "product_to_duo_matrix": product_to_duo_matrix}


def standardize_features(x):
    mean = lax.optimization_barrier(jnp.mean(x, axis=-1, keepdims=True))
    centred = x - mean
    var = lax.optimization_barrier(jnp.mean(centred * centred, axis=-1, keepdims=True))
    return centred * lax.rsqrt(var + 1e-05)

def reference(alignment_tensor, amino_exists_flags, chain_exists_flags, chosen_slab_number, duo_tensor, duo_offset_matrix, asking_matrix, lookup_matrix, content_matrix, sigmoid_matrix, final_projection_matrix, first_factor_matrix, second_factor_matrix, product_to_duo_matrix):
    normed_pair = standardize_features(duo_tensor.astype(jnp.float32)).astype(jnp.bfloat16)
    bias = jnp.einsum('ijc,ch->hij', normed_pair.astype(jnp.float32), duo_offset_matrix.astype(jnp.float32)).astype(jnp.bfloat16)
    bias_wide = bias.astype(jnp.float32)
    standardized_alignment = standardize_features(alignment_tensor.astype(jnp.float32)).astype(jnp.bfloat16).reshape(ALIGN_CHAINS * AMINO_COUNT, ALIGN_FEATURES)
    asking_vector = jnp.dot(standardized_alignment, asking_matrix, preferred_element_type=jnp.float32).astype(jnp.bfloat16).reshape(ALIGN_CHAINS, AMINO_COUNT, SCORE_GROUPS, GROUP_FEATURES)
    key = jnp.dot(standardized_alignment, lookup_matrix, preferred_element_type=jnp.float32).astype(jnp.bfloat16).reshape(ALIGN_CHAINS, AMINO_COUNT, SCORE_GROUPS, GROUP_FEATURES)
    content_vector = jnp.dot(standardized_alignment, content_matrix, preferred_element_type=jnp.float32).astype(jnp.bfloat16).reshape(ALIGN_CHAINS, AMINO_COUNT, SCORE_GROUPS, GROUP_FEATURES)
    sigmoid_argument = jnp.dot(standardized_alignment, sigmoid_matrix, preferred_element_type=jnp.float32).reshape(ALIGN_CHAINS, AMINO_COUNT, SCORE_GROUPS * GROUP_FEATURES)
    scale = 1.0 / GROUP_FEATURES ** 0.5

    def one_sequence(items):
        q_seq, k_seq, v_seq, m_seq = items
        score = jnp.einsum('ihd,jhd->hij', q_seq.astype(jnp.float32), k_seq.astype(jnp.float32)) * scale + bias_wide
        score = jnp.where(m_seq[None, None, :] > 0, score, -1000000000.0)
        probs = jax.nn.softmax(score, axis=-1).astype(jnp.bfloat16)
        out = jnp.einsum('hij,jhd->ihd', probs.astype(jnp.float32), v_seq.astype(jnp.float32))
        return out.astype(jnp.bfloat16)
    probability_combined = lax.map(one_sequence, (asking_vector, key, content_vector, amino_exists_flags))
    scaled_heads = (jax.nn.sigmoid(sigmoid_argument) * probability_combined.reshape(ALIGN_CHAINS, AMINO_COUNT, SCORE_GROUPS * GROUP_FEATURES).astype(jnp.float32)).astype(jnp.bfloat16)
    duo_increment = jnp.dot(scaled_heads.reshape(ALIGN_CHAINS * AMINO_COUNT, SCORE_GROUPS * GROUP_FEATURES), final_projection_matrix, preferred_element_type=jnp.float32).reshape(ALIGN_CHAINS, AMINO_COUNT, ALIGN_FEATURES)
    alignment_reweighted = (alignment_tensor.astype(jnp.float32) + duo_increment).astype(jnp.bfloat16)
    standardized_newer = standardize_features(alignment_reweighted.astype(jnp.float32)).astype(jnp.bfloat16).reshape(ALIGN_CHAINS * AMINO_COUNT, ALIGN_FEATURES)
    retained_flags = chain_exists_flags.astype(jnp.float32)[:, None, None]
    first_factor = (jnp.dot(standardized_newer, first_factor_matrix, preferred_element_type=jnp.float32).reshape(ALIGN_CHAINS, AMINO_COUNT, PROJECTED_WIDTH) * retained_flags).astype(jnp.bfloat16)
    second_factor = (jnp.dot(standardized_newer, second_factor_matrix, preferred_element_type=jnp.float32).reshape(ALIGN_CHAINS, AMINO_COUNT, PROJECTED_WIDTH) * retained_flags).astype(jnp.bfloat16)
    start = (chosen_slab_number[0] * SLAB).astype(jnp.int32)
    first_factor_slice = lax.dynamic_slice_in_dim(first_factor, start, SLAB, 1)
    tensor_product = jnp.einsum('dnw,dgr->ngwr', first_factor_slice.astype(jnp.float32), second_factor.astype(jnp.float32)) / ALIGN_CHAINS
    tensor_product = tensor_product.astype(jnp.bfloat16).reshape(SLAB * AMINO_COUNT, PROJECTED_WIDTH * PROJECTED_WIDTH)
    product_average = jnp.dot(tensor_product, product_to_duo_matrix, preferred_element_type=jnp.float32).reshape(SLAB, AMINO_COUNT, DUO_FEATURES).astype(jnp.bfloat16)
    return (alignment_reweighted, product_average)
```

```python
import functools

import jax
import jax.numpy as jnp
from jax import lax
from jax.experimental import pallas as pl
from jax.experimental.pallas import tpu as pltpu
from jax.sharding import PartitionSpec as P

LOG2E = 1.4426950408889634
MASKED = -1e9 * LOG2E
BOTH = ("row", "col")
NT = (((1,), (1,)), ((), ()))
TN = (((0,), (0,)), ((), ()))


def dot(a, b, dims=None):
    if dims is None:
        return jnp.dot(a, b, preferred_element_type=jnp.float32)
    return lax.dot_general(a, b, dims, preferred_element_type=jnp.float32)


def params(mib=48):
    return pltpu.CompilerParams(vmem_limit_bytes=mib << 20)


def cost(flops, moved, exps=0):
    return pl.CostEstimate(flops=flops, bytes_accessed=moved, transcendentals=exps)


def standardize(x):
    mean = jnp.mean(x, axis=-1, keepdims=True)
    centred = x - mean
    var = jnp.mean(centred * centred, axis=-1, keepdims=True)
    return centred * lax.rsqrt(var + 1e-05)


def iota(shape, dim):
    return lax.broadcasted_iota(jnp.int32, shape, dim)


def spread_columns(w):
    row, col = iota((256, 1024), 0), iota((256, 1024), 1)
    pick = (row == (col // 128) * 32 + col % 32).astype(jnp.bfloat16)
    wide = dot(w, pick).astype(jnp.bfloat16)
    quarter = (col // 32) % 4
    return [jnp.where(quarter == si, wide, jnp.zeros_like(wide)) for si in range(4)]


def spread_rows(w):
    row, col = iota((1024, 256), 0), iota((1024, 256), 1)
    pick = (col == (row // 128) * 32 + row % 32).astype(jnp.bfloat16)
    tall = dot(pick, w).astype(jnp.bfloat16)
    quarter = (row // 32) % 4
    return [jnp.where(quarter == si, tall, jnp.zeros_like(tall)) for si in range(4)]


def factor_columns(w, residue):
    row, col = iota((32, 256), 0), iota((32, 256), 1)
    pick = jnp.where((row == col // 8) & (col % 8 == residue), 1.0, 0.0).astype(jnp.bfloat16)
    return dot(w, pick).astype(jnp.bfloat16)


def right_columns(w, residue):
    row, col = iota((32, 256), 0), iota((32, 256), 1)
    pick = jnp.where((row == col % 32) & (col // 32 == residue), 1.0, 0.0).astype(jnp.bfloat16)
    return dot(w, pick).astype(jnp.bfloat16)


def four_abreast(x):
    groups, width = x.shape[0], x.shape[3]
    return jnp.concatenate([x[:, si].reshape(groups * 8, width) for si in range(4)], axis=1)


def bias_kernel(duo_ref, w_ref, flags_ref, out_ref, rows_s):
    step = pl.program_id(0)

    @pl.when(step < 4)
    def _():
        x = duo_ref[...].reshape(16 * 128, 128).astype(jnp.float32)
        n = standardize(x).astype(jnp.bfloat16)
        heads = lax.dot_general(
            w_ref[...], n, (((0,), (1,)), ((), ())), preferred_element_type=jnp.float32
        )
        for i in range(16):
            rows_s[:, i, :] = heads[:, i * 128 : (i + 1) * 128] * LOG2E
        out_ref[...] = rows_s[...].astype(jnp.bfloat16)

    @pl.when(step == 4)
    def _():
        out_ref[...] = jnp.broadcast_to(flags_ref[...][None], (8, 16, 128))


def bias_tile(duo, w, flags):
    return pl.pallas_call(
        bias_kernel,
        grid=(5,),
        in_specs=[
            pl.BlockSpec((16, 128, 128), lambda i: (jnp.minimum(i, 3), 0, 0)),
            pl.BlockSpec((128, 8), lambda i: (0, 0)),
            pl.BlockSpec((16, 128), lambda i: (0, 0)),
        ],
        out_specs=pl.BlockSpec((8, 16, 128), lambda i: (0, i, 0)),
        out_shape=jax.ShapeDtypeStruct((8, 80, 128), jnp.bfloat16),
        scratch_shapes=[pltpu.VMEM((8, 16, 128), jnp.float32)],
        compiler_params=params(),
        cost_estimate=cost(20_000_000, 2_200_000),
        name="bias_tile",
    )(duo, w, flags)


def qkv_kernel(x_ref, wq_ref, wk_ref, wv_ref, out_ref, w_s):
    @pl.when(pl.program_id(0) == 0)
    def _():
        for t, w in enumerate((wq_ref, wk_ref, wv_ref)):
            for si, part in enumerate(spread_columns(w[...])):
                w_s[t, si * 256 : (si + 1) * 256, :] = part

    x = x_ref[...].reshape(16, 4, 8, 256).astype(jnp.float32)
    n = four_abreast(standardize(x)).astype(jnp.bfloat16)
    for t in range(3):
        y = dot(n, w_s[t])
        if t == 0:
            y = y * (LOG2E / 32**0.5)
        y = y.reshape(4, 4, 8, 1024)
        for h in range(8):
            for g in range(4):
                out_ref[h, t, g] = y[:, g, :, h * 128 : (h + 1) * 128].astype(jnp.bfloat16)


def qkv(x, wq, wk, wv):
    whole = pl.BlockSpec((256, 256), lambda i: (0, 0))
    return pl.pallas_call(
        qkv_kernel,
        grid=(4,),
        in_specs=[
            pl.BlockSpec((4, 4, 4, 8, 256), lambda i: (i, 0, 0, 0, 0)),
            whole,
            whole,
            whole,
        ],
        out_specs=pl.BlockSpec((8, 3, 4, 4, 8, 128), lambda i: (0, 0, 0, i, 0, 0)),
        out_shape=jax.ShapeDtypeStruct((8, 3, 4, 16, 8, 128), jnp.bfloat16),
        scratch_shapes=[pltpu.VMEM((3, 1024, 1024), jnp.bfloat16)],
        compiler_params=params(),
        cost_estimate=cost(3_500_000_000, 4_500_000),
        name="qkv",
    )(x, wq, wk, wv)


def natural(block):
    x = jnp.swapaxes(block.astype(jnp.float32), 0, 1)
    return x.reshape(x.shape[0] * 64, 128).astype(jnp.bfloat16)


def attention_kernel(
    block, blocks, slab_ref, q_ref, k_ref, v_ref, bias_ref, mask_ref, out_ref, q_s, k_s, v_s
):
    lane = iota((1, 128), 1) // 32
    q_s[...] = natural(q_ref[:, 0, 0])
    k_s[...] = natural(k_ref[:, 0, 0])
    v = natural(v_ref[:, 0, 0])
    for si in range(4):
        keep = lane == si
        v_s[si, :, :128] = jnp.where(keep, v, jnp.zeros_like(v))
        v_s[si, :, 128:] = jnp.broadcast_to(jnp.where(keep, 1.0, 0.0), (1024, 128)).astype(
            jnp.bfloat16
        )
    present = [mask_ref[0, si : si + 1, :] > 0 for si in range(4)]
    tiles = block // 64

    def step(at, carry):
        rows = pl.ds(pl.multiple_of(at * block, block), block)
        q = q_s[rows, :]
        bias = jnp.concatenate(
            [
                jnp.concatenate([bias_ref[at * tiles + t, c, :64, :] for c in range(8)], 1)
                for t in range(tiles)
            ],
            0,
        )
        total = jnp.zeros((block, 256), jnp.float32)
        for si in range(4):
            one = jnp.where(lane == si, q, jnp.zeros_like(q))
            score = dot(one, k_s[...], NT) + bias.astype(jnp.float32)
            score = jnp.where(present[si], score, MASKED)
            top = jnp.max(score, axis=1, keepdims=True)
            probs = jnp.exp2(score - top).astype(jnp.bfloat16)
            total = total + dot(probs, v_s[si])
        result = total[:, :128] / total[:, 128:]
        eighth = block // 8
        out_ref[pl.ds(pl.multiple_of(at * eighth, eighth), eighth), 0] = result.reshape(
            eighth, 8, 128
        ).astype(jnp.bfloat16)
        return carry

    lax.fori_loop(0, blocks, step, 0)


def attention(received, bias, mask, slab=None):
    if slab is None:
        block, count = 256, 16
        slab = jnp.zeros((1,), jnp.int32)
        first = lambda slab_ref: 0
        name = "attention"
    else:
        block, count = 64, 1
        first = lambda slab_ref: slab_ref[0]
        name = "slab_attention"
    part = lambda t: pl.BlockSpec((8, 1, 1, 16, 8, 128), lambda g, s: (0, t, g, 0, 0, 0))
    return pl.pallas_call(
        functools.partial(attention_kernel, block, count * 64 // block),
        grid_spec=pltpu.PrefetchScalarGridSpec(
            num_scalar_prefetch=1,
            grid=(4,),
            in_specs=[
                pl.BlockSpec((8, 1, 1, count, 8, 128), lambda g, s: (0, 0, g, first(s), 0, 0)),
                part(1),
                part(2),
                pl.BlockSpec((count, 8, 80, 128), lambda g, s: (first(s), 0, 0, 0)),
                pl.BlockSpec((1, 4, 1024), lambda g, s: (g, 0, 0)),
            ],
            out_specs=pl.BlockSpec((count * 8, 1, 8, 128), lambda g, s: (0, g, 0, 0)),
            scratch_shapes=[
                pltpu.VMEM((count * 64, 128), jnp.bfloat16),
                pltpu.VMEM((1024, 128), jnp.bfloat16),
                pltpu.VMEM((4, 1024, 256), jnp.bfloat16),
            ],
        ),
        out_shape=jax.ShapeDtypeStruct((count * 8, 4, 8, 128), jnp.bfloat16),
        compiler_params=params(),
        cost_estimate=cost(count * 2_000_000_000, 3_000_000 + count * 200_000, count << 20),
        name=name,
    )(slab, received, received, received, bias, mask)


def gated_update(x, weighted, w_gate, w_out):
    n = four_abreast(standardize(x)).astype(jnp.bfloat16)
    gate = jax.nn.sigmoid(dot(n, w_gate))
    gated = (gate * weighted).astype(jnp.bfloat16)
    update = dot(gated, w_out)
    fresh = x + jnp.stack(
        [update[:, si * 256 : (si + 1) * 256].reshape(-1, 8, 256) for si in range(4)], axis=1
    )
    return fresh.astype(jnp.bfloat16).astype(jnp.float32)


def fill_weights(gate_ref, out_ref, gate_s, out_s):
    for si, part in enumerate(spread_columns(gate_ref[...])):
        gate_s[si * 256 : (si + 1) * 256, :] = part
    for si, part in enumerate(spread_rows(out_ref[...])):
        out_s[:, si * 256 : (si + 1) * 256] = part


def left_kernel(
    slab_ref, x_ref, weighted_ref, flags_ref, gate_ref, out_w_ref, factor_ref, out_ref,
    gate_s, out_s, normed_s,
):
    fill_weights(gate_ref, out_w_ref, gate_s, out_s)
    x = x_ref[0].astype(jnp.float32)
    weighted = jnp.concatenate(
        [weighted_ref[h].astype(jnp.float32).reshape(32, 128) for h in range(8)], axis=1
    )
    fresh = gated_update(x, weighted, gate_s[...], out_s[...])
    normed_s[...] = standardize(fresh).reshape(16, 8, 256)
    left = jnp.zeros((16, 256), jnp.float32)
    for residue in range(8):
        part = normed_s[:, residue, :].astype(jnp.bfloat16)
        left = left + dot(part, factor_columns(factor_ref[...], residue))
    left = (left * flags_ref[...]).astype(jnp.bfloat16)
    out_ref[...] = jnp.broadcast_to(left[None], (128, 16, 256))


def left_factor(slab, x, weighted, flags, w_gate, w_out, w_first):
    whole = lambda *shape: pl.BlockSpec(shape, lambda i, s: (0,) * len(shape))
    return pl.pallas_call(
        left_kernel,
        grid_spec=pltpu.PrefetchScalarGridSpec(
            num_scalar_prefetch=1,
            grid=(1,),
            in_specs=[
                pl.BlockSpec((1, 4, 4, 8, 256), lambda i, s: (s[0], 0, 0, 0, 0)),
                whole(8, 4, 8, 128),
                whole(16, 1),
                whole(256, 256),
                whole(256, 256),
                whole(256, 32),
            ],
            out_specs=whole(128, 16, 256),
            scratch_shapes=[
                pltpu.VMEM((1024, 1024), jnp.bfloat16),
                pltpu.VMEM((1024, 1024), jnp.bfloat16),
                pltpu.VMEM((16, 8, 256), jnp.float32),
            ],
        ),
        out_shape=jax.ShapeDtypeStruct((128, 16, 256), jnp.bfloat16),
        compiler_params=params(),
        cost_estimate=cost(1_000_000_000, 1_500_000),
        name="left_factor",
    )(slab, x, weighted, flags, w_gate, w_out, w_first)


def final_kernel(
    x_ref, weighted_ref, flags_ref, left_ref, gate_ref, out_w_ref, factor_ref, product_ref,
    fresh_ref, pair_ref, gate_s, out_s, factor_s, normed_s, right_s, outer_s, pair_s,
):
    step = pl.program_id(0)

    @pl.when(step == 0)
    def _():
        fill_weights(gate_ref, out_w_ref, gate_s, out_s)
        for residue in range(8):
            factor_s[residue] = right_columns(factor_ref[...], residue)

    x = x_ref[...].reshape(16, 4, 8, 256).astype(jnp.float32)
    weighted = jnp.concatenate(
        [
            weighted_ref[:, h].astype(jnp.float32).reshape(128, 128)
            for h in range(8)
        ],
        axis=1,
    )
    fresh = gated_update(x, weighted, gate_s[...], out_s[...])
    fresh_ref[...] = fresh.reshape(64, 8, 256).astype(jnp.bfloat16)
    normed_s[...] = standardize(fresh).reshape(64, 8, 256)
    right = jnp.zeros((64, 256), jnp.float32)
    for residue in range(8):
        part = normed_s[:, residue, :].astype(jnp.bfloat16)
        right = right + dot(part, factor_s[residue])
    right_s[pl.ds(pl.multiple_of(step * 64, 64), 64), :] = (right * flags_ref[...]).astype(
        jnp.bfloat16
    )

    @pl.when(step == pl.num_programs(0) - 1)
    def _():
        right_all = right_s[...]
        for c in range(8):
            left = left_ref[:, c].reshape(256, 256)
            outer_s[:, c] = (dot(left, right_all, TN) * (1.0 / 256)).reshape(32, 8, 256)
        lane = iota((1, 128), 1) // 32
        for j in range(8):
            half, source = (j // 4) * 128, j % 4
            quads = []
            for quad in range(8):
                block = None
                for u in range(4):
                    part = outer_s[quad * 4 + u, :, :, half : half + 128].reshape(64, 128)
                    if u != source:
                        part = pltpu.roll(part, ((u - source) % 4) * 32, 1)
                    block = part if block is None else jnp.where(lane == u, part, block)
                quads.append(block.astype(jnp.bfloat16))
            pair_s[:, j, :] = dot(jnp.concatenate(quads, axis=1), product_ref[...])
        pair_ref[...] = pair_s[...].astype(jnp.bfloat16)


def finish(x, weighted, flags, left, w_gate, w_out, w_second, w_product):
    whole = lambda *shape: pl.BlockSpec(shape, lambda i: (0,) * len(shape))
    return pl.pallas_call(
        final_kernel,
        grid=(4,),
        in_specs=[
            pl.BlockSpec((64, 8, 256), lambda i: (i, 0, 0)),
            pl.BlockSpec((4, 8, 4, 8, 128), lambda i: (i, 0, 0, 0, 0)),
            pl.BlockSpec((64, 1), lambda i: (i, 0)),
            whole(16, 8, 16, 256),
            whole(256, 256),
            whole(256, 256),
            whole(256, 32),
            whole(1024, 128),
        ],
        out_specs=[pl.BlockSpec((64, 8, 256), lambda i: (i, 0, 0)), whole(64, 8, 128)],
        out_shape=[
            jax.ShapeDtypeStruct((256, 8, 256), jnp.bfloat16),
            jax.ShapeDtypeStruct((64, 8, 128), jnp.bfloat16),
        ],
        scratch_shapes=[
            pltpu.VMEM((1024, 1024), jnp.bfloat16),
            pltpu.VMEM((1024, 1024), jnp.bfloat16),
            pltpu.VMEM((8, 256, 256), jnp.bfloat16),
            pltpu.VMEM((64, 8, 256), jnp.float32),
            pltpu.VMEM((256, 256), jnp.bfloat16),
            pltpu.VMEM((32, 8, 8, 256), jnp.float32),
            pltpu.VMEM((64, 8, 128), jnp.float32),
        ],
        compiler_params=params(),
        cost_estimate=cost(3_000_000_000, 5_000_000),
        name="finish",
    )(x, weighted, flags, left, w_gate, w_out, w_second, w_product)


def exchange(x, axes):
    return lax.all_to_all(x, axes, split_axis=0, concat_axis=0, tiled=True)


def per_device(
    alignment_tensor,
    amino_exists_flags,
    chain_exists_flags,
    chosen_slab_number,
    duo_tensor,
    duo_offset_matrix,
    asking_matrix,
    lookup_matrix,
    content_matrix,
    sigmoid_matrix,
    final_projection_matrix,
    first_factor_matrix,
    second_factor_matrix,
    product_to_duo_matrix,
):
    row = lax.axis_index("row")
    slab = chosen_slab_number
    sequences = exchange(alignment_tensor, "row").reshape(16, 4, 4, 8, 256)
    flags = amino_exists_flags.astype(jnp.bfloat16).reshape(16, 128)
    tile = bias_tile(duo_tensor, duo_offset_matrix, flags)
    bias = lax.all_gather(exchange(tile, "col"), "row", axis=0, tiled=False)
    received = exchange(qkv(sequences, asking_matrix, lookup_matrix, content_matrix), "col")

    mask = lax.dynamic_index_in_dim(bias, 64 + row, axis=2, keepdims=False)
    mask = jnp.transpose(mask.reshape(16, 8, 16, 8), (2, 0, 1, 3))
    mask = mask.reshape(4, 4, 1024).astype(jnp.float32)

    chains = chain_exists_flags.astype(jnp.float32)[:, None]
    own_chains = lax.dynamic_slice_in_dim(chains, row * 16, 16, 0)
    slab_weighted = exchange(attention(received, bias, mask, slab), "col")
    left = left_factor(
        slab,
        sequences,
        slab_weighted,
        own_chains,
        sigmoid_matrix,
        final_projection_matrix,
        first_factor_matrix,
    )
    left = exchange(left, BOTH).reshape(16, 8, 16, 256)
    weighted = exchange(attention(received, bias, mask), BOTH).reshape(16, 8, 4, 8, 128)
    return tuple(
        finish(
            alignment_tensor,
            weighted,
            chains,
            left,
            sigmoid_matrix,
            final_projection_matrix,
            second_factor_matrix,
            product_to_duo_matrix,
        )
    )


def solution(mesh):
    placed = (
        P(None, BOTH, None),
        P(None, BOTH),
        P(),
        P(),
        P("row", "col", None),
    ) + (P(),) * 9
    return jax.shard_map(
        per_device,
        mesh=mesh,
        in_specs=placed,
        out_specs=(P(None, BOTH, None), P(None, BOTH, None)),
        check_vma=False,
    )
```

```python
import functools

import jax
import jax.numpy as jnp
from jax import lax
from jax.experimental import pallas as pl
from jax.experimental.pallas import tpu as pltpu
from jax.sharding import PartitionSpec as P

LOG2E = 1.4426950408889634
MASKED = -1e9 * LOG2E
ROW = ("xl", "y", "core")
COL = ("xh", "z")
BOTH = ROW + COL
BLOCK, UNROLL = 256, 4
NT = (((1,), (1,)), ((), ()))
TN = (((0,), (0,)), ((), ()))


def dot(a, b, dims=None):
    if dims is None:
        return jnp.dot(a, b, preferred_element_type=jnp.float32)
    return lax.dot_general(a, b, dims, preferred_element_type=jnp.float32)


def params(mib=60):
    return pltpu.CompilerParams(vmem_limit_bytes=mib << 20)


def cost(flops, moved, exps=0):
    return pl.CostEstimate(flops=flops, bytes_accessed=moved, transcendentals=exps)


def standardize(x):
    mean = jnp.mean(x, axis=-1, keepdims=True)
    centred = x - mean
    var = jnp.mean(centred * centred, axis=-1, keepdims=True)
    return centred * lax.rsqrt(var + 1e-05)


def iota(shape, dim):
    return lax.broadcasted_iota(jnp.int32, shape, dim)


def spread_columns(w):
    row, col = iota((256, 1024), 0), iota((256, 1024), 1)
    pick = (row == (col // 128) * 32 + col % 32).astype(jnp.bfloat16)
    wide = dot(w, pick).astype(jnp.bfloat16)
    quarter = (col // 32) % 4
    return [jnp.where(quarter == si, wide, jnp.zeros_like(wide)) for si in range(4)]


def spread_rows(w):
    row, col = iota((1024, 256), 0), iota((1024, 256), 1)
    pick = (col == (row // 128) * 32 + row % 32).astype(jnp.bfloat16)
    tall = dot(pick, w).astype(jnp.bfloat16)
    quarter = (row // 32) % 4
    return [jnp.where(quarter == si, tall, jnp.zeros_like(tall)) for si in range(4)]


def factor_columns(w, residue):
    row, col = iota((32, 256), 0), iota((32, 256), 1)
    pick = jnp.where((row == col // 8) & (col % 8 == residue), 1.0, 0.0).astype(jnp.bfloat16)
    return dot(w, pick).astype(jnp.bfloat16)


def right_columns(w, residue):
    row, col = iota((32, 256), 0), iota((32, 256), 1)
    pick = jnp.where((row == col % 32) & (col // 32 == residue), 1.0, 0.0).astype(jnp.bfloat16)
    return dot(w, pick).astype(jnp.bfloat16)


def four_abreast(x):
    groups, width = x.shape[0], x.shape[3]
    return jnp.concatenate([x[:, si].reshape(groups * 8, width) for si in range(4)], axis=1)


def bias_kernel(duo_ref, w_ref, flags_ref, out_ref, rows_s):
    step = pl.program_id(0)

    @pl.when(step < 4)
    def _():
        x = duo_ref[...].reshape(16 * 128, 128).astype(jnp.float32)
        n = standardize(x).astype(jnp.bfloat16)
        heads = lax.dot_general(
            w_ref[...], n, (((0,), (1,)), ((), ())), preferred_element_type=jnp.float32
        )
        for i in range(16):
            rows_s[:, i, :] = heads[:, i * 128 : (i + 1) * 128] * LOG2E
        out_ref[...] = jnp.broadcast_to(rows_s[...].astype(jnp.bfloat16)[None], (2, 8, 16, 128))

    @pl.when(step == 4)
    def _():
        out_ref[...] = jnp.broadcast_to(flags_ref[...][None, None], (2, 8, 16, 128))


def bias_tile(duo, w, flags):
    return pl.pallas_call(
        bias_kernel,
        grid=(5,),
        in_specs=[
            pl.BlockSpec((16, 128, 128), lambda i: (jnp.minimum(i, 3), 0, 0)),
            pl.BlockSpec((128, 8), lambda i: (0, 0)),
            pl.BlockSpec((16, 128), lambda i: (0, 0)),
        ],
        out_specs=pl.BlockSpec((2, 8, 16, 128), lambda i: (0, 0, i, 0)),
        out_shape=jax.ShapeDtypeStruct((2, 8, 80, 128), jnp.bfloat16),
        scratch_shapes=[pltpu.VMEM((8, 16, 128), jnp.float32)],
        compiler_params=params(),
        cost_estimate=cost(20_000_000, 2_200_000),
        name="bias_tile",
    )(duo, w, flags)


def qkv_kernel(x_ref, wq_ref, wk_ref, wv_ref, early_ref, late_ref, w_s):
    @pl.when(pl.program_id(0) == 0)
    def _():
        for t, w in enumerate((wq_ref, wk_ref, wv_ref)):
            for si, part in enumerate(spread_columns(w[...])):
                w_s[t, si * 256 : (si + 1) * 256, :] = part

    x = x_ref[...].reshape(16, 4, 8, 256).astype(jnp.float32)
    n = four_abreast(standardize(x)).astype(jnp.bfloat16)
    for t in range(3):
        y = dot(n, w_s[t])
        if t == 0:
            y = y * (LOG2E / 32**0.5)
        y = y.reshape(4, 4, 8, 1024)
        for h in range(8):
            for g in range(4):
                out_ref = early_ref if g < 2 else late_ref
                out_ref[h, t, g % 2] = y[:, g, :, h * 128 : (h + 1) * 128].astype(jnp.bfloat16)


def qkv(x, wq, wk, wv):
    whole = pl.BlockSpec((256, 256), lambda i: (0, 0))
    return pl.pallas_call(
        qkv_kernel,
        grid=(4,),
        in_specs=[
            pl.BlockSpec((4, 4, 4, 8, 256), lambda i: (i, 0, 0, 0, 0)),
            whole,
            whole,
            whole,
        ],
        out_specs=[pl.BlockSpec((8, 3, 2, 4, 8, 128), lambda i: (0, 0, 0, i, 0, 0))] * 2,
        out_shape=[jax.ShapeDtypeStruct((8, 3, 2, 16, 8, 128), jnp.bfloat16)] * 2,
        scratch_shapes=[pltpu.VMEM((3, 1024, 1024), jnp.bfloat16)],
        compiler_params=params(),
        cost_estimate=cost(3_500_000_000, 4_500_000),
        name="qkv",
    )(x, wq, wk, wv)


def natural(block):
    x = jnp.swapaxes(block.astype(jnp.float32), 0, 1)
    return x.reshape(x.shape[0] * 64, 128).astype(jnp.bfloat16)


def bias_tile_at(bias_ref, r, c):
    if bias_ref.shape[0] == 1:
        return bias_ref[0, 0, c, :64, :]
    return bias_ref[lax.rem(r, 8), lax.div(r, 8), c, :64, :]


def attend(block, blocks, q_ref, k_ref, v_ref, bias_ref, present, out_ref, q_s, k_s, v_s):
    lane = iota((1, 128), 1) // 32
    wide_lane = (iota((1, 256), 1) // 32) % 4
    q_s[...] = natural(q_ref[:, 0, 0])
    k_s[...] = natural(k_ref[:, 0, 0])
    v_s[:, :128] = natural(v_ref[:, 0, 0])

    @pl.when(pl.program_id(0) == 0)
    def _():
        v_s[:, 128:] = jnp.ones((1024, 128), jnp.bfloat16)

    tiles = block // 64

    def step(at, carry):
        rows = pl.ds(pl.multiple_of(at * block, block), block)
        q = q_s[rows, :]
        bias = jnp.concatenate(
            [
                jnp.concatenate([bias_tile_at(bias_ref, at * tiles + t, c) for c in range(8)], 1)
                for t in range(tiles)
            ],
            0,
        ).astype(jnp.float32)
        ones = [jnp.where(lane == si, q, jnp.zeros_like(q)) for si in range(4)]

        def probs(score, si):
            score = jnp.where(present[si : si + 1] > 0, score + bias, MASKED)
            top = jnp.max(score, axis=1, keepdims=True)
            return jnp.exp2(score - top).astype(jnp.bfloat16)

        if block > 64:
            parts = [dot(probs(dot(ones[si], k_s[...], NT), si), v_s[...]) for si in range(4)]
        else:
            scores = dot(jnp.concatenate(ones, 0), k_s[...], NT)
            parts = [probs(scores[si * block : (si + 1) * block], si) for si in range(4)]
            parts = dot(jnp.concatenate(parts, 0), v_s[...])
            parts = [parts[si * block : (si + 1) * block] for si in range(4)]
        total = parts[0]
        for si in range(1, 4):
            total = jnp.where(wide_lane == si, parts[si], total)
        result = total[:, :128] / total[:, 128:]
        eighth = block // 8
        out_ref[pl.ds(pl.multiple_of(at * eighth, eighth), eighth), 0, 0] = result.reshape(
            eighth, 8, 128
        ).astype(jnp.bfloat16)
        return carry

    lax.fori_loop(0, blocks, step, 0, unroll=min(UNROLL, blocks))


def first_kernel(
    at_ref, q_ref, k_ref, v_ref, bias_ref, flags_ref, out_ref, slab_ref, mask_ref, *scratch
):
    @pl.when(pl.program_id(0) == 0)
    def _():
        both = flags_ref[...].astype(jnp.float32)
        flags = jnp.where(at_ref[1] // 8 == 0, both[..., :8, :], both[..., 8:, :])
        flags = jnp.swapaxes(flags, 0, 1)
        own = iota((16, 128), 1) == (at_ref[1] % 8) * 16 + iota((16, 128), 0)
        mask = dot(own.astype(jnp.bfloat16), flags.reshape(1024, 128).astype(jnp.bfloat16), NT)
        for g in range(4):
            mask_ref[g] = mask[g * 4 : g * 4 + 4]

    present = mask_ref[pl.program_id(0)]
    attend(BLOCK, 1024 // BLOCK, q_ref, k_ref, v_ref, bias_ref, present, out_ref, *scratch)
    slab_ref[:, 0, 0] = out_ref[pl.ds(pl.multiple_of(at_ref[0] * 8, 8), 8), 0, 0]


def slab_kernel(at_ref, q_ref, k_ref, v_ref, bias_ref, mask_ref, _, out_ref, *scratch):
    attend(64, 1, q_ref, k_ref, v_ref, bias_ref, mask_ref[0], out_ref, *scratch)


def later_kernel(q_ref, k_ref, v_ref, bias_ref, mask_ref, *rest):
    attend(BLOCK, 1024 // BLOCK, q_ref, k_ref, v_ref, bias_ref, mask_ref[0], *rest[-4:])


def attention_scratch(rows):
    return [
        pltpu.VMEM((rows, 128), jnp.bfloat16),
        pltpu.VMEM((1024, 128), jnp.bfloat16),
        pltpu.VMEM((1024, 256), jnp.bfloat16),
    ]


RETURNED = jax.ShapeDtypeStruct((128, 2, 4, 8, 128), jnp.bfloat16)
SLAB_WEIGHTED = jax.ShapeDtypeStruct((8, 1, 4, 8, 128), jnp.bfloat16)


def first_attention(at, received, bias):
    part = lambda t: pl.BlockSpec((8, 1, 1, 16, 8, 128), lambda g, s: (0, t, g, 0, 0, 0))
    return pl.pallas_call(
        first_kernel,
        grid_spec=pltpu.PrefetchScalarGridSpec(
            num_scalar_prefetch=1,
            grid=(2,),
            in_specs=[
                part(0),
                part(1),
                part(2),
                pl.BlockSpec((8, 2, 8, 80, 128), lambda g, s: (0, 0, 0, 0, 0)),
                pl.BlockSpec((8, 2, 8, 16, 128), lambda g, s: (0, 0, 0, 4, 0)),
            ],
            out_specs=[
                pl.BlockSpec((128, 1, 1, 8, 128), lambda g, s: (0, 0, g, 0, 0)),
                pl.BlockSpec((8, 1, 1, 8, 128), lambda g, s: (0, 0, g, 0, 0)),
                pl.BlockSpec((4, 4, 1024), lambda g, s: (0, 0, 0)),
            ],
            scratch_shapes=attention_scratch(1024),
        ),
        out_shape=[RETURNED, SLAB_WEIGHTED, jax.ShapeDtypeStruct((4, 4, 1024), jnp.float32)],
        compiler_params=params(),
        cost_estimate=cost(16_000_000_000, 4_000_000, 2 << 22),
        name="first_attention",
    )(at, received, received, received, bias, bias)


def slab_attention(at, received, bias, mask, onto):
    part = lambda t: pl.BlockSpec((8, 1, 1, 16, 8, 128), lambda g, s: (0, t, g, 0, 0, 0))
    return pl.pallas_call(
        slab_kernel,
        grid_spec=pltpu.PrefetchScalarGridSpec(
            num_scalar_prefetch=1,
            grid=(2,),
            in_specs=[
                pl.BlockSpec((8, 1, 1, 1, 8, 128), lambda g, s: (0, 0, g, s[0], 0, 0)),
                part(1),
                part(2),
                pl.BlockSpec(
                    (1, 1, 8, 80, 128), lambda g, s: (lax.rem(s[0], 8), lax.div(s[0], 8), 0, 0, 0)
                ),
                pl.BlockSpec((1, 4, 1024), lambda g, s: (g + 2, 0, 0)),
                pl.BlockSpec(memory_space=pl.ANY),
            ],
            out_specs=pl.BlockSpec((8, 1, 1, 8, 128), lambda g, s: (0, 0, g + 2, 0, 0)),
            scratch_shapes=attention_scratch(64),
        ),
        out_shape=SLAB_WEIGHTED,
        input_output_aliases={6: 0},
        compiler_params=params(),
        cost_estimate=cost(1_000_000_000, 2_000_000, 1 << 19),
        name="slab_attention",
    )(at, received, received, received, bias, mask, onto)


def later_attention(received, bias, mask, onto):
    part = lambda t: pl.BlockSpec((8, 1, 1, 16, 8, 128), lambda g: (0, t, g, 0, 0, 0))
    return pl.pallas_call(
        later_kernel,
        grid=(2,),
        in_specs=[
            part(0),
            part(1),
            part(2),
            pl.BlockSpec((8, 2, 8, 80, 128), lambda g: (0, 0, 0, 0, 0)),
            pl.BlockSpec((1, 4, 1024), lambda g: (g + 2, 0, 0)),
            pl.BlockSpec(memory_space=pl.ANY),
        ],
        out_specs=pl.BlockSpec((128, 1, 1, 8, 128), lambda g: (0, 0, g + 2, 0, 0)),
        out_shape=RETURNED,
        scratch_shapes=attention_scratch(1024),
        input_output_aliases={5: 0},
        compiler_params=params(),
        cost_estimate=cost(16_000_000_000, 4_000_000, 2 << 22),
        name="later_attention",
    )(received, received, received, bias, mask, onto)


def gates(x, w):
    return jax.nn.sigmoid(dot(four_abreast(standardize(x)).astype(jnp.bfloat16), w))


def prepare_kernel(
    at_ref, x_ref, slab_ref, gate_ref, out_w_ref, gates_ref, slab_gates_ref, spread_ref, w_s
):
    @pl.when(pl.program_id(0) == 0)
    def _():
        for si, part in enumerate(spread_columns(gate_ref[...])):
            w_s[si * 256 : (si + 1) * 256, :] = part
        for si, part in enumerate(spread_rows(out_w_ref[...])):
            spread_ref[:, si * 256 : (si + 1) * 256] = part
        slab_gates_ref[...] = gates(slab_ref[0].astype(jnp.float32), w_s[...])

    x = x_ref[...].reshape(16, 4, 8, 256).astype(jnp.float32)
    gates_ref[...] = gates(x, w_s[...]).astype(jnp.bfloat16)


def prepare(at, x, sequences, w_gate, w_out):
    whole = lambda *shape: pl.BlockSpec(shape, lambda i, s: (0,) * len(shape))
    return pl.pallas_call(
        prepare_kernel,
        grid_spec=pltpu.PrefetchScalarGridSpec(
            num_scalar_prefetch=1,
            grid=(4,),
            in_specs=[
                pl.BlockSpec((64, 8, 256), lambda i, s: (i, 0, 0)),
                pl.BlockSpec((1, 4, 4, 8, 256), lambda i, s: (s[0], 0, 0, 0, 0)),
                whole(256, 256),
                whole(256, 256),
            ],
            out_specs=[
                pl.BlockSpec((128, 1024), lambda i, s: (i, 0)),
                whole(32, 1024),
                whole(1024, 1024),
            ],
            scratch_shapes=[pltpu.VMEM((1024, 1024), jnp.bfloat16)],
        ),
        out_shape=[
            jax.ShapeDtypeStruct((512, 1024), jnp.bfloat16),
            jax.ShapeDtypeStruct((32, 1024), jnp.float32),
            jax.ShapeDtypeStruct((1024, 1024), jnp.bfloat16),
        ],
        compiler_params=params(),
        cost_estimate=cost(1_500_000_000, 6_000_000),
        name="prepare",
    )(at, x, sequences, w_gate, w_out)


def gated_update(x, gate, weighted, w_out):
    gated = (gate * weighted).astype(jnp.bfloat16)
    update = dot(gated, w_out)
    fresh = x + jnp.stack(
        [update[:, si * 256 : (si + 1) * 256].reshape(-1, 8, 256) for si in range(4)], axis=1
    )
    return fresh.astype(jnp.bfloat16).astype(jnp.float32)


def left_kernel(
    at_ref, x_ref, weighted_ref, flags_ref, gate_ref, out_w_ref, factor_ref, _, out_ref, normed_s
):
    x = x_ref[0].astype(jnp.float32)
    weighted = jnp.concatenate(
        [weighted_ref[h, 0].astype(jnp.float32).reshape(32, 128) for h in range(8)], axis=1
    )
    fresh = gated_update(x, gate_ref[...], weighted, out_w_ref[...])
    normed_s[...] = standardize(fresh).reshape(16, 8, 256)
    left = jnp.zeros((16, 256), jnp.float32)
    for residue in range(8):
        part = normed_s[:, residue, :].astype(jnp.bfloat16)
        left = left + dot(part, factor_columns(factor_ref[...], residue))
    left = left * flags_ref[...]
    for half in range(2):
        part = left[:, half * 128 : (half + 1) * 128].reshape(1, 2, 8, 128).astype(jnp.bfloat16)
        out_ref[:, 0, 2 * half : 2 * half + 2] = jnp.broadcast_to(part, (128, 2, 8, 128))


def left_factor(at, x, weighted, flags, gate, w_out, w_first, onto):
    whole = lambda *shape: pl.BlockSpec(shape, lambda i, s: (0,) * len(shape))
    return pl.pallas_call(
        left_kernel,
        grid_spec=pltpu.PrefetchScalarGridSpec(
            num_scalar_prefetch=1,
            grid=(1,),
            in_specs=[
                pl.BlockSpec((1, 4, 4, 8, 256), lambda i, s: (s[0], 0, 0, 0, 0)),
                whole(8, 1, 4, 8, 128),
                whole(16, 1),
                whole(32, 1024),
                whole(1024, 1024),
                whole(256, 32),
                pl.BlockSpec(memory_space=pl.ANY),
            ],
            out_specs=pl.BlockSpec((128, 1, 4, 8, 128), lambda i, s: (0, 1, 0, 0, 0)),
            scratch_shapes=[pltpu.VMEM((16, 8, 256), jnp.float32)],
        ),
        out_shape=RETURNED,
        input_output_aliases={7: 0},
        compiler_params=params(),
        cost_estimate=cost(100_000_000, 3_500_000),
        name="left_factor",
    )(at, x, weighted, flags, gate, w_out, w_first, onto)


def final_kernel(
    x_ref, weighted_ref, flags_ref, left_ref, gate_ref, out_w_ref, factor_ref, product_ref,
    fresh_ref, pair_ref, factor_s, normed_s, right_s, outer_s, pair_s,
):
    step = pl.program_id(0)

    @pl.when(step == 0)
    def _():
        for residue in range(8):
            factor_s[residue] = right_columns(factor_ref[...], residue)

    x = x_ref[...].reshape(16, 4, 8, 256).astype(jnp.float32)
    weighted = jnp.concatenate(
        [
            weighted_ref[:, h, 0].astype(jnp.float32).reshape(128, 128)
            for h in range(8)
        ],
        axis=1,
    )
    fresh = gated_update(x, gate_ref[...].astype(jnp.float32), weighted, out_w_ref[...])
    fresh_ref[...] = fresh.reshape(64, 8, 256).astype(jnp.bfloat16)
    normed_s[...] = standardize(fresh).reshape(64, 8, 256)
    right = jnp.zeros((64, 256), jnp.float32)
    for residue in range(8):
        part = normed_s[:, residue, :].astype(jnp.bfloat16)
        right = right + dot(part, factor_s[residue])
    right_s[pl.ds(pl.multiple_of(step * 64, 64), 64), :] = (right * flags_ref[...]).astype(
        jnp.bfloat16
    )

    @pl.when(step == pl.num_programs(0) - 1)
    def _():
        right_all = right_s[...]
        for c in range(8):
            left = left_ref[:, c, 0].astype(jnp.float32)
            left = jnp.concatenate(
                [left[:, :2].reshape(256, 128), left[:, 2:].reshape(256, 128)], axis=1
            ).astype(jnp.bfloat16)
            outer_s[:, c] = (dot(left, right_all, TN) * (1.0 / 256)).reshape(32, 8, 256)
        lane = iota((1, 128), 1) // 32
        for j in range(8):
            half, source = (j // 4) * 128, j % 4
            quads = []
            for quad in range(8):
                block = None
                for u in range(4):
                    part = outer_s[quad * 4 + u, :, :, half : half + 128].reshape(64, 128)
                    if u != source:
                        part = pltpu.roll(part, ((u - source) % 4) * 32, 1)
                    block = part if block is None else jnp.where(lane == u, part, block)
                quads.append(block.astype(jnp.bfloat16))
            pair_s[:, j, :] = dot(jnp.concatenate(quads, axis=1), product_ref[...])
        pair_ref[...] = pair_s[...].astype(jnp.bfloat16)


def finish(x, returned, flags, gate, w_out, w_second, w_product):
    whole = lambda *shape: pl.BlockSpec(shape, lambda i: (0,) * len(shape))
    return pl.pallas_call(
        final_kernel,
        grid=(4,),
        in_specs=[
            pl.BlockSpec((64, 8, 256), lambda i: (i, 0, 0)),
            pl.BlockSpec((4, 8, 1, 4, 8, 128), lambda i: (i, 0, 0, 0, 0, 0)),
            pl.BlockSpec((64, 1), lambda i: (i, 0)),
            pl.BlockSpec((16, 8, 1, 4, 8, 128), lambda i: (0, 0, 1, 0, 0, 0)),
            pl.BlockSpec((128, 1024), lambda i: (i, 0)),
            whole(1024, 1024),
            whole(256, 32),
            whole(1024, 128),
        ],
        out_specs=[pl.BlockSpec((64, 8, 256), lambda i: (i, 0, 0)), whole(64, 8, 128)],
        out_shape=[
            jax.ShapeDtypeStruct((256, 8, 256), jnp.bfloat16),
            jax.ShapeDtypeStruct((64, 8, 128), jnp.bfloat16),
        ],
        scratch_shapes=[
            pltpu.VMEM((8, 256, 256), jnp.bfloat16),
            pltpu.VMEM((64, 8, 256), jnp.float32),
            pltpu.VMEM((256, 256), jnp.bfloat16),
            pltpu.VMEM((32, 8, 8, 256), jnp.float32),
            pltpu.VMEM((64, 8, 128), jnp.float32),
        ],
        compiler_params=params(),
        cost_estimate=cost(3_000_000_000, 5_000_000),
        name="finish",
    )(x, returned, flags, returned, gate, w_out, w_second, w_product)


def exchange(x, axes):
    return lax.all_to_all(x, axes, split_axis=0, concat_axis=0, tiled=True)


def per_device(
    alignment_tensor,
    amino_exists_flags,
    chain_exists_flags,
    chosen_slab_number,
    duo_tensor,
    duo_offset_matrix,
    asking_matrix,
    lookup_matrix,
    content_matrix,
    sigmoid_matrix,
    final_projection_matrix,
    first_factor_matrix,
    second_factor_matrix,
    product_to_duo_matrix,
):
    row = lax.axis_index(ROW)
    at = jnp.concatenate([chosen_slab_number, jnp.reshape(row, (1,)).astype(jnp.int32)])
    sequences = exchange(alignment_tensor, ROW).reshape(16, 4, 4, 8, 256)

    flags = jnp.transpose(amino_exists_flags.reshape(2, 128, 8), (0, 2, 1))
    flags = flags.reshape(16, 128).astype(jnp.bfloat16)
    tile = bias_tile(duo_tensor, duo_offset_matrix, flags)
    sequences, tile = lax.optimization_barrier((sequences, tile))
    tile = exchange(tile.reshape(16, 80, 128), ("xl",) + COL)
    early, late = qkv(sequences, asking_matrix, lookup_matrix, content_matrix)
    early, late, tile = lax.optimization_barrier((early, late, tile))
    bias = lax.all_gather(tile.reshape(2, 8, 80, 128), ("y", "core"), axis=0, tiled=False)
    early = exchange(early, COL)
    late, early = lax.optimization_barrier((late, early))
    late = exchange(late, COL)

    chains = chain_exists_flags.astype(jnp.float32)[:, None]
    own_chains = lax.dynamic_slice_in_dim(chains, row * 16, 16, 0)
    gate, slab_gate, w_out = prepare(
        at, alignment_tensor, sequences, sigmoid_matrix, final_projection_matrix
    )

    early, gate, slab_gate, w_out = lax.optimization_barrier((early, gate, slab_gate, w_out))
    returned, slab_weighted, mask = first_attention(at, early, bias)
    slab_weighted = slab_attention(at, late, bias, mask, slab_weighted)
    slab_weighted = exchange(slab_weighted, COL)
    returned = later_attention(late, bias, mask, returned)
    slab_weighted, returned = lax.optimization_barrier((slab_weighted, returned))
    returned = left_factor(
        at, sequences, slab_weighted, own_chains, slab_gate, w_out, first_factor_matrix, returned
    )
    returned = exchange(returned, BOTH)
    return tuple(
        finish(
            alignment_tensor,
            returned.reshape(16, 8, 2, 4, 8, 128),
            chains,
            gate,
            w_out,
            second_factor_matrix,
            product_to_duo_matrix,
        )
    )


def solution(mesh):
    mesh = jax.sharding.Mesh(mesh.devices.reshape(2, 4, 2, 2, 4), BOTH)
    placed = (
        P(None, BOTH, None),
        P(None, BOTH),
        P(),
        P(),
        P(ROW, COL, None),
    ) + (P(),) * 9
    return jax.shard_map(
        per_device,
        mesh=mesh,
        in_specs=placed,
        out_specs=(P(None, BOTH, None), P(None, BOTH, None)),
        check_vma=False,
    )
```

```python
import functools

import jax
import jax.numpy as jnp
from jax import lax
from jax.experimental import pallas as pl
from jax.experimental.pallas import tpu as pltpu
from jax.sharding import PartitionSpec as P

LOG2E = 1.4426950408889634
MASKED = -1e9 * LOG2E
ROW = ("xl", "y", "core")
COL = ("xh", "z")
BOTH = ROW + COL
BLOCK, UNROLL = 256, 4
QKV_STEPS, FINISH_STEPS = 2, 1
NT = (((1,), (1,)), ((), ()))
TN = (((0,), (0,)), ((), ()))


def dot(a, b, dims=None):
    if dims is None:
        return jnp.dot(a, b, preferred_element_type=jnp.float32)
    return lax.dot_general(a, b, dims, preferred_element_type=jnp.float32)


def params(mib=60):
    return pltpu.CompilerParams(vmem_limit_bytes=mib << 20)


def cost(flops, moved, exps=0):
    return pl.CostEstimate(flops=flops, bytes_accessed=moved, transcendentals=exps)


def standardize(x):
    mean = jnp.mean(x, axis=-1, keepdims=True)
    centred = x - mean
    var = jnp.mean(centred * centred, axis=-1, keepdims=True)
    return centred * lax.rsqrt(var + 1e-05)


def iota(shape, dim):
    return lax.broadcasted_iota(jnp.int32, shape, dim)


def factor(normed, w, across):
    row, col = iota((32, 256), 0), iota((32, 256), 1)
    channel, residue = (col % 32, col // 32) if across == 32 else (col // 8, col % 8)
    wide = dot(w, (row == channel).astype(jnp.bfloat16)).astype(jnp.bfloat16)
    y = dot(normed, wide).reshape(-1, 8, 256)
    own = iota((1, 8, 256), 1) == residue[:1].reshape(1, 1, 256)
    return jnp.sum(jnp.where(own, y, 0.0), axis=1)


def swap_quarters(blocks):
    quarter = iota((1, 128), 1) // 32

    def swap(a, b, shift, keep):
        return (
            jnp.where(keep, a, pltpu.roll(b, shift, 1)),
            jnp.where(keep, pltpu.roll(a, 128 - shift, 1), b),
        )

    a, b, c, d = blocks
    a, c = swap(a, c, 64, quarter < 2)
    b, d = swap(b, d, 64, quarter < 2)
    a, b = swap(a, b, 32, quarter % 2 == 0)
    c, d = swap(c, d, 32, quarter % 2 == 0)
    return a, b, c, d


def by_sequence(heads):
    first, second = swap_quarters(heads[:4]), swap_quarters(heads[4:])
    whole = [jnp.concatenate(two, axis=1).reshape(-1, 8, 256) for two in zip(first, second)]
    return jnp.stack(whole, axis=1).reshape(-1, 256)


def by_head(y):
    y = y.reshape(-1, 4, 8, 256)
    heads = []
    for half in range(2):
        blocks = [y[:, si, :, half * 128 : (half + 1) * 128].reshape(-1, 128) for si in range(4)]
        heads.extend(swap_quarters(blocks))
    return heads


def bias_kernel(duo_ref, w_ref, flags_ref, out_ref, rows_s):
    step = pl.program_id(0)

    @pl.when(step < 4)
    def _():
        x = duo_ref[...].reshape(16 * 128, 128).astype(jnp.float32)
        n = standardize(x).astype(jnp.bfloat16)
        heads = lax.dot_general(
            w_ref[...], n, (((0,), (1,)), ((), ())), preferred_element_type=jnp.float32
        )
        for i in range(16):
            rows_s[:, i, :] = heads[:, i * 128 : (i + 1) * 128] * LOG2E
        out_ref[...] = jnp.broadcast_to(rows_s[...].astype(jnp.bfloat16)[None], (2, 8, 16, 128))

    @pl.when(step == 4)
    def _():
        out_ref[...] = jnp.broadcast_to(flags_ref[...][None, None], (2, 8, 16, 128))


def bias_tile(duo, w, flags):
    return pl.pallas_call(
        bias_kernel,
        grid=(5,),
        in_specs=[
            pl.BlockSpec((16, 128, 128), lambda i: (jnp.minimum(i, 3), 0, 0)),
            pl.BlockSpec((128, 8), lambda i: (0, 0)),
            pl.BlockSpec((16, 128), lambda i: (0, 0)),
        ],
        out_specs=pl.BlockSpec((2, 8, 16, 128), lambda i: (0, 0, i, 0)),
        out_shape=jax.ShapeDtypeStruct((2, 8, 80, 128), jnp.bfloat16),
        scratch_shapes=[pltpu.VMEM((8, 16, 128), jnp.float32)],
        compiler_params=params(),
        cost_estimate=cost(20_000_000, 2_200_000),
        name="bias_tile",
    )(duo, w, flags)


def qkv_kernel(x_ref, wq_ref, wk_ref, wv_ref, early_ref, late_ref):
    groups = 16 // QKV_STEPS
    n = standardize(x_ref[...].reshape(groups * 128, 256).astype(jnp.float32))
    n = n.astype(jnp.bfloat16)
    for t, w in enumerate((wq_ref, wk_ref, wv_ref)):
        y = dot(n, w[...])
        if t == 0:
            y = y * (LOG2E / 32**0.5)
        for h, part in enumerate(by_head(y)):
            part = part.reshape(groups, 4, 8, 128).astype(jnp.bfloat16)
            for g in range(4):
                out_ref = early_ref if g < 2 else late_ref
                out_ref[h, t, g % 2] = part[:, g]


def qkv(x, wq, wk, wv):
    whole = pl.BlockSpec((256, 256), lambda i: (0, 0))
    return pl.pallas_call(
        qkv_kernel,
        grid=(QKV_STEPS,),
        in_specs=[
            pl.BlockSpec((16 // QKV_STEPS, 4, 4, 8, 256), lambda i: (i, 0, 0, 0, 0)),
            whole,
            whole,
            whole,
        ],
        out_specs=[pl.BlockSpec((8, 3, 2, 16 // QKV_STEPS, 8, 128), lambda i: (0, 0, 0, i, 0, 0))] * 2,
        out_shape=[jax.ShapeDtypeStruct((8, 3, 2, 16, 8, 128), jnp.bfloat16)] * 2,
        compiler_params=params(),
        cost_estimate=cost(800_000_000, 4_500_000),
        name="qkv",
    )(x, wq, wk, wv)


def natural(block):
    x = jnp.swapaxes(block.astype(jnp.float32), 0, 1)
    return x.reshape(x.shape[0] * 64, 128).astype(jnp.bfloat16)


def bias_tile_at(bias_ref, r, c):
    if bias_ref.shape[0] == 1:
        return bias_ref[0, 0, c, :64, :]
    return bias_ref[lax.rem(r, 8), lax.div(r, 8), c, :64, :]


def attend(block, blocks, q_ref, k_ref, v_ref, bias_ref, present, out_ref, q_s, k_s, v_s):
    lane = iota((1, 128), 1) // 32
    wide_lane = (iota((1, 256), 1) // 32) % 4
    q_s[...] = natural(q_ref[:, 0, 0])
    k_s[...] = natural(k_ref[:, 0, 0])
    v_s[:, :128] = natural(v_ref[:, 0, 0])

    @pl.when(pl.program_id(0) == 0)
    def _():
        v_s[:, 128:] = jnp.ones((1024, 128), jnp.bfloat16)

    tiles = block // 64

    def step(at, carry):
        rows = pl.ds(pl.multiple_of(at * block, block), block)
        q = q_s[rows, :]
        bias = jnp.concatenate(
            [
                jnp.concatenate([bias_tile_at(bias_ref, at * tiles + t, c) for c in range(8)], 1)
                for t in range(tiles)
            ],
            0,
        ).astype(jnp.float32)
        ones = [jnp.where(lane == si, q, jnp.zeros_like(q)) for si in range(4)]

        def probs(score, si):
            score = jnp.where(present[si : si + 1] > 0, score + bias, MASKED)
            top = jnp.max(score, axis=1, keepdims=True)
            return jnp.exp2(score - top).astype(jnp.bfloat16)

        if block > 64:
            parts = [dot(probs(dot(ones[si], k_s[...], NT), si), v_s[...]) for si in range(4)]
        else:
            scores = dot(jnp.concatenate(ones, 0), k_s[...], NT)
            parts = [probs(scores[si * block : (si + 1) * block], si) for si in range(4)]
            parts = dot(jnp.concatenate(parts, 0), v_s[...])
            parts = [parts[si * block : (si + 1) * block] for si in range(4)]
        total = parts[0]
        for si in range(1, 4):
            total = jnp.where(wide_lane == si, parts[si], total)
        result = total[:, :128] / total[:, 128:]
        eighth = block // 8
        out_ref[pl.ds(pl.multiple_of(at * eighth, eighth), eighth), 0, 0] = result.reshape(
            eighth, 8, 128
        ).astype(jnp.bfloat16)
        return carry

    lax.fori_loop(0, blocks, step, 0, unroll=min(UNROLL, blocks))


def first_kernel(
    at_ref, q_ref, k_ref, v_ref, bias_ref, flags_ref, out_ref, slab_ref, slab_bias_ref, mask_ref, *scratch
):
    @pl.when(pl.program_id(0) == 0)
    def _():
        both = flags_ref[...].astype(jnp.float32)
        flags = jnp.where(at_ref[1] // 8 == 0, both[..., :8, :], both[..., 8:, :])
        flags = jnp.swapaxes(flags, 0, 1)
        own = iota((16, 128), 1) == (at_ref[1] % 8) * 16 + iota((16, 128), 0)
        mask = dot(own.astype(jnp.bfloat16), flags.reshape(1024, 128).astype(jnp.bfloat16), NT)
        for g in range(4):
            mask_ref[g] = mask[g * 4 : g * 4 + 4]
        slab = at_ref[0]
        slab_bias_ref[0, 0] = bias_ref[lax.rem(slab, 8), lax.div(slab, 8), :, :64]

    present = mask_ref[pl.program_id(0)]
    attend(BLOCK, 1024 // BLOCK, q_ref, k_ref, v_ref, bias_ref, present, out_ref, *scratch)
    slab_ref[:, 0, 0] = out_ref[pl.ds(pl.multiple_of(at_ref[0] * 8, 8), 8), 0, 0]


def slab_kernel(at_ref, q_ref, k_ref, v_ref, bias_ref, mask_ref, _, out_ref, *scratch):
    attend(64, 1, q_ref, k_ref, v_ref, bias_ref, mask_ref[0], out_ref, *scratch)


def later_kernel(q_ref, k_ref, v_ref, bias_ref, mask_ref, *rest):
    attend(BLOCK, 1024 // BLOCK, q_ref, k_ref, v_ref, bias_ref, mask_ref[0], *rest[-4:])


def attention_scratch(rows):
    return [
        pltpu.VMEM((rows, 128), jnp.bfloat16),
        pltpu.VMEM((1024, 128), jnp.bfloat16),
        pltpu.VMEM((1024, 256), jnp.bfloat16),
    ]


RETURNED = jax.ShapeDtypeStruct((128, 2, 4, 8, 128), jnp.bfloat16)
SLAB_WEIGHTED = jax.ShapeDtypeStruct((8, 1, 4, 8, 128), jnp.bfloat16)


def first_attention(at, received, bias):
    part = lambda t: pl.BlockSpec((8, 1, 1, 16, 8, 128), lambda g, s: (0, t, g, 0, 0, 0))
    return pl.pallas_call(
        first_kernel,
        grid_spec=pltpu.PrefetchScalarGridSpec(
            num_scalar_prefetch=1,
            grid=(2,),
            in_specs=[
                part(0),
                part(1),
                part(2),
                pl.BlockSpec((8, 2, 8, 80, 128), lambda g, s: (0, 0, 0, 0, 0)),
                pl.BlockSpec((8, 2, 8, 16, 128), lambda g, s: (0, 0, 0, 4, 0)),
            ],
            out_specs=[
                pl.BlockSpec((128, 1, 1, 8, 128), lambda g, s: (0, 0, g, 0, 0)),
                pl.BlockSpec((8, 1, 1, 8, 128), lambda g, s: (0, 0, g, 0, 0)),
                pl.BlockSpec((1, 1, 8, 64, 128), lambda g, s: (0, 0, 0, 0, 0)),
                pl.BlockSpec((4, 4, 1024), lambda g, s: (0, 0, 0)),
            ],
            scratch_shapes=attention_scratch(1024),
        ),
        out_shape=[
            RETURNED,
            SLAB_WEIGHTED,
            jax.ShapeDtypeStruct((1, 1, 8, 64, 128), jnp.bfloat16),
            jax.ShapeDtypeStruct((4, 4, 1024), jnp.float32),
        ],
        compiler_params=params(),
        cost_estimate=cost(16_000_000_000, 4_000_000, 2 << 22),
        name="first_attention",
    )(at, received, received, received, bias, bias)


def slab_attention(at, received, bias, mask, onto):
    part = lambda t: pl.BlockSpec((8, 1, 1, 16, 8, 128), lambda g, s: (0, t, g, 0, 0, 0))
    return pl.pallas_call(
        slab_kernel,
        grid_spec=pltpu.PrefetchScalarGridSpec(
            num_scalar_prefetch=1,
            grid=(2,),
            in_specs=[
                pl.BlockSpec((8, 1, 1, 1, 8, 128), lambda g, s: (0, 0, g, s[0], 0, 0)),
                part(1),
                part(2),
                pl.BlockSpec((1, 1, 8, 64, 128), lambda g, s: (0, 0, 0, 0, 0)),
                pl.BlockSpec((1, 4, 1024), lambda g, s: (g + 2, 0, 0)),
                pl.BlockSpec(memory_space=pl.ANY),
            ],
            out_specs=pl.BlockSpec((8, 1, 1, 8, 128), lambda g, s: (0, 0, g + 2, 0, 0)),
            scratch_shapes=attention_scratch(64),
        ),
        out_shape=SLAB_WEIGHTED,
        input_output_aliases={6: 0},
        compiler_params=params(),
        cost_estimate=cost(1_000_000_000, 2_000_000, 1 << 19),
        name="slab_attention",
    )(at, received, received, received, bias, mask, onto)


def later_attention(received, bias, mask, onto):
    part = lambda t: pl.BlockSpec((8, 1, 1, 16, 8, 128), lambda g: (0, t, g, 0, 0, 0))
    return pl.pallas_call(
        later_kernel,
        grid=(2,),
        in_specs=[
            part(0),
            part(1),
            part(2),
            pl.BlockSpec((8, 2, 8, 80, 128), lambda g: (0, 0, 0, 0, 0)),
            pl.BlockSpec((1, 4, 1024), lambda g: (g + 2, 0, 0)),
            pl.BlockSpec(memory_space=pl.ANY),
        ],
        out_specs=pl.BlockSpec((128, 1, 1, 8, 128), lambda g: (0, 0, g + 2, 0, 0)),
        out_shape=RETURNED,
        scratch_shapes=attention_scratch(1024),
        input_output_aliases={5: 0},
        compiler_params=params(),
        cost_estimate=cost(16_000_000_000, 4_000_000, 2 << 22),
        name="later_attention",
    )(received, received, received, bias, mask, onto)


def gates(x, w):
    return jax.nn.sigmoid(dot(standardize(x).astype(jnp.bfloat16), w))


def prepare_kernel(at_ref, x_ref, slab_ref, gate_ref, gates_ref, slab_gates_ref):
    x = x_ref[...].reshape(2048, 256).astype(jnp.float32)
    gates_ref[...] = gates(x, gate_ref[...]).astype(jnp.bfloat16)
    slab_gates_ref[...] = gates(slab_ref[0].reshape(128, 256).astype(jnp.float32), gate_ref[...])


def prepare(at, x, sequences, w_gate):
    whole = lambda *shape: pl.BlockSpec(shape, lambda i, s: (0,) * len(shape))
    return pl.pallas_call(
        prepare_kernel,
        grid_spec=pltpu.PrefetchScalarGridSpec(
            num_scalar_prefetch=1,
            grid=(1,),
            in_specs=[
                whole(256, 8, 256),
                pl.BlockSpec((1, 4, 4, 8, 256), lambda i, s: (s[0], 0, 0, 0, 0)),
                whole(256, 256),
            ],
            out_specs=[whole(2048, 256), whole(128, 256)],
        ),
        out_shape=[
            jax.ShapeDtypeStruct((2048, 256), jnp.bfloat16),
            jax.ShapeDtypeStruct((128, 256), jnp.float32),
        ],
        compiler_params=params(),
        cost_estimate=cost(300_000_000, 3_000_000),
        name="prepare",
    )(at, x, sequences, w_gate)


def gated_update(x, gate, heads, w_out):
    gated = (gate * by_sequence(heads)).astype(jnp.bfloat16)
    return (x + dot(gated, w_out)).astype(jnp.bfloat16).astype(jnp.float32)


def left_kernel(
    at_ref, x_ref, weighted_ref, flags_ref, gate_ref, out_w_ref, factor_ref, _, out_ref
):
    x = x_ref[0].reshape(128, 256).astype(jnp.float32)
    heads = [weighted_ref[h, 0].astype(jnp.float32).reshape(32, 128) for h in range(8)]
    fresh = gated_update(x, gate_ref[...], heads, out_w_ref[...])
    left = factor(standardize(fresh).astype(jnp.bfloat16), factor_ref[...], 1)
    left = left * flags_ref[...]
    for half in range(2):
        part = left[:, half * 128 : (half + 1) * 128].reshape(1, 2, 8, 128).astype(jnp.bfloat16)
        out_ref[:, 0, 2 * half : 2 * half + 2] = jnp.broadcast_to(part, (128, 2, 8, 128))


def left_factor(at, x, weighted, flags, gate, w_out, w_first, onto):
    whole = lambda *shape: pl.BlockSpec(shape, lambda i, s: (0,) * len(shape))
    return pl.pallas_call(
        left_kernel,
        grid_spec=pltpu.PrefetchScalarGridSpec(
            num_scalar_prefetch=1,
            grid=(1,),
            in_specs=[
                pl.BlockSpec((1, 4, 4, 8, 256), lambda i, s: (s[0], 0, 0, 0, 0)),
                whole(8, 1, 4, 8, 128),
                whole(16, 1),
                whole(128, 256),
                whole(256, 256),
                whole(256, 32),
                pl.BlockSpec(memory_space=pl.ANY),
            ],
            out_specs=pl.BlockSpec((128, 1, 4, 8, 128), lambda i, s: (0, 1, 0, 0, 0)),
        ),
        out_shape=RETURNED,
        input_output_aliases={7: 0},
        compiler_params=params(),
        cost_estimate=cost(100_000_000, 3_500_000),
        name="left_factor",
    )(at, x, weighted, flags, gate, w_out, w_first, onto)


def final_kernel(
    x_ref, weighted_ref, flags_ref, left_ref, gate_ref, out_w_ref, factor_ref, product_ref,
    fresh_ref, pair_ref, right_s, outer_s, pair_s,
):
    step = pl.program_id(0)
    chains = 256 // FINISH_STEPS

    x = x_ref[...].reshape(chains * 8, 256).astype(jnp.float32)
    heads = [
        weighted_ref[:, h, 0].astype(jnp.float32).reshape(chains * 2, 128) for h in range(8)
    ]
    fresh = gated_update(x, gate_ref[...].astype(jnp.float32), heads, out_w_ref[...])
    fresh_ref[...] = fresh.reshape(chains, 8, 256).astype(jnp.bfloat16)
    right = factor(standardize(fresh).astype(jnp.bfloat16), factor_ref[...], 32)
    right_s[pl.ds(pl.multiple_of(step * chains, chains), chains), :] = (right * flags_ref[...]).astype(
        jnp.bfloat16
    )

    @pl.when(step == pl.num_programs(0) - 1)
    def _():
        right_all = right_s[...]
        for c in range(8):
            left = left_ref[:, c, 0].astype(jnp.float32)
            left = jnp.concatenate(
                [left[:, :2].reshape(256, 128), left[:, 2:].reshape(256, 128)], axis=1
            ).astype(jnp.bfloat16)
            outer_s[:, c] = (dot(left, right_all, TN) * (1.0 / 256)).reshape(32, 8, 256)
        lane = iota((1, 128), 1) // 32
        for j in range(8):
            half, source = (j // 4) * 128, j % 4
            quads = []
            for quad in range(8):
                block = None
                for u in range(4):
                    part = outer_s[quad * 4 + u, :, :, half : half + 128].reshape(64, 128)
                    if u != source:
                        part = pltpu.roll(part, ((u - source) % 4) * 32, 1)
                    block = part if block is None else jnp.where(lane == u, part, block)
                quads.append(block.astype(jnp.bfloat16))
            pair_s[:, j, :] = dot(jnp.concatenate(quads, axis=1), product_ref[...])
        pair_ref[...] = pair_s[...].astype(jnp.bfloat16)


def finish(x, returned, flags, gate, w_out, w_second, w_product):
    whole = lambda *shape: pl.BlockSpec(shape, lambda i: (0,) * len(shape))
    return pl.pallas_call(
        final_kernel,
        grid=(FINISH_STEPS,),
        in_specs=[
            pl.BlockSpec((256 // FINISH_STEPS, 8, 256), lambda i: (i, 0, 0)),
            pl.BlockSpec((16 // FINISH_STEPS, 8, 1, 4, 8, 128), lambda i: (i, 0, 0, 0, 0, 0)),
            pl.BlockSpec((256 // FINISH_STEPS, 1), lambda i: (i, 0)),
            pl.BlockSpec((16, 8, 1, 4, 8, 128), lambda i: (0, 0, 1, 0, 0, 0)),
            pl.BlockSpec((2048 // FINISH_STEPS, 256), lambda i: (i, 0)),
            whole(256, 256),
            whole(256, 32),
            whole(1024, 128),
        ],
        out_specs=[pl.BlockSpec((256 // FINISH_STEPS, 8, 256), lambda i: (i, 0, 0)), whole(64, 8, 128)],
        out_shape=[
            jax.ShapeDtypeStruct((256, 8, 256), jnp.bfloat16),
            jax.ShapeDtypeStruct((64, 8, 128), jnp.bfloat16),
        ],
        scratch_shapes=[
            pltpu.VMEM((256, 256), jnp.bfloat16),
            pltpu.VMEM((32, 8, 8, 256), jnp.float32),
            pltpu.VMEM((64, 8, 128), jnp.float32),
        ],
        compiler_params=params(36),
        cost_estimate=cost(3_000_000_000, 5_000_000),
        name="finish",
    )(x, returned, flags, returned, gate, w_out, w_second, w_product)


def exchange(x, axes):
    return lax.all_to_all(x, axes, split_axis=0, concat_axis=0, tiled=True)


def per_device(
    alignment_tensor,
    amino_exists_flags,
    chain_exists_flags,
    chosen_slab_number,
    duo_tensor,
    duo_offset_matrix,
    asking_matrix,
    lookup_matrix,
    content_matrix,
    sigmoid_matrix,
    final_projection_matrix,
    first_factor_matrix,
    second_factor_matrix,
    product_to_duo_matrix,
):
    row = lax.axis_index(ROW)
    at = jnp.concatenate([chosen_slab_number, jnp.reshape(row, (1,)).astype(jnp.int32)])
    sequences = exchange(alignment_tensor, ROW).reshape(16, 4, 4, 8, 256)

    flags = jnp.transpose(amino_exists_flags.reshape(2, 128, 8), (0, 2, 1))
    flags = flags.reshape(16, 128).astype(jnp.bfloat16)
    tile = bias_tile(duo_tensor, duo_offset_matrix, flags)
    sequences, tile = lax.optimization_barrier((sequences, tile))
    tile = exchange(tile.reshape(16, 80, 128), ("xl",) + COL)
    early, late = qkv(sequences, asking_matrix, lookup_matrix, content_matrix)
    early, late, tile = lax.optimization_barrier((early, late, tile))
    bias = lax.all_gather(tile.reshape(2, 8, 80, 128), ("y", "core"), axis=0, tiled=False)
    early = exchange(early, COL)
    late, early = lax.optimization_barrier((late, early))
    late = exchange(late, COL)

    chains = chain_exists_flags.astype(jnp.float32)[:, None]
    own_chains = lax.dynamic_slice_in_dim(chains, row * 16, 16, 0)
    gate, slab_gate = prepare(at, alignment_tensor, sequences, sigmoid_matrix)

    early, gate, slab_gate = lax.optimization_barrier((early, gate, slab_gate))
    returned, slab_weighted, slab_bias, mask = first_attention(at, early, bias)
    slab_weighted = slab_attention(at, late, slab_bias, mask, slab_weighted)
    slab_weighted = exchange(slab_weighted, COL)
    returned = later_attention(late, bias, mask, returned)
    slab_weighted, returned = lax.optimization_barrier((slab_weighted, returned))
    returned = left_factor(
        at,
        sequences,
        slab_weighted,
        own_chains,
        slab_gate,
        final_projection_matrix,
        first_factor_matrix,
        returned,
    )
    returned = exchange(returned, BOTH)
    return tuple(
        finish(
            alignment_tensor,
            returned.reshape(16, 8, 2, 4, 8, 128),
            chains,
            gate,
            final_projection_matrix,
            second_factor_matrix,
            product_to_duo_matrix,
        )
    )


def solution(mesh):
    mesh = jax.sharding.Mesh(mesh.devices.reshape(2, 4, 2, 2, 4), BOTH)
    placed = (
        P(None, BOTH, None),
        P(None, BOTH),
        P(),
        P(),
        P(ROW, COL, None),
    ) + (P(),) * 9
    return jax.shard_map(
        per_device,
        mesh=mesh,
        in_specs=placed,
        out_specs=(P(None, BOTH, None), P(None, BOTH, None)),
        check_vma=False,
    )
```

```python
import functools

import jax
import jax.numpy as jnp
from jax import lax
from jax.experimental import pallas as pl
from jax.experimental.pallas import tpu as pltpu
from jax.sharding import PartitionSpec as P

LOG2E = 1.4426950408889634
MASKED = -1e9 * LOG2E
ROW = ("xl", "y", "core")
COL = ("xh", "z")
BOTH = ROW + COL
BLOCK, UNROLL = 256, 4
QKV_STEPS = 2
NT = (((1,), (1,)), ((), ()))
TN = (((0,), (0,)), ((), ()))


def dot(a, b, dims=None):
    if dims is None:
        return jnp.dot(a, b, preferred_element_type=jnp.float32)
    return lax.dot_general(a, b, dims, preferred_element_type=jnp.float32)


def params(mib=60):
    return pltpu.CompilerParams(vmem_limit_bytes=mib << 20)


def cost(flops, moved, exps=0):
    return pl.CostEstimate(flops=flops, bytes_accessed=moved, transcendentals=exps)


def standardize(x):
    mean = jnp.mean(x, axis=-1, keepdims=True)
    centred = x - mean
    var = jnp.mean(centred * centred, axis=-1, keepdims=True)
    return centred * lax.rsqrt(var + 1e-05)


def iota(shape, dim):
    return lax.broadcasted_iota(jnp.int32, shape, dim)


def factor(normed, w, across):
    row, col = iota((32, 256), 0), iota((32, 256), 1)
    channel, residue = (col % 32, col // 32) if across == 32 else (col // 8, col % 8)
    wide = dot(w, (row == channel).astype(jnp.bfloat16)).astype(jnp.bfloat16)
    y = dot(normed, wide).reshape(-1, 8, 256)
    own = iota((1, 8, 256), 1) == residue[:1].reshape(1, 1, 256)
    return jnp.sum(jnp.where(own, y, 0.0), axis=1)


def swap_quarters(blocks):
    quarter = iota((1, 128), 1) // 32

    def swap(a, b, shift, keep):
        return (
            jnp.where(keep, a, pltpu.roll(b, shift, 1)),
            jnp.where(keep, pltpu.roll(a, 128 - shift, 1), b),
        )

    a, b, c, d = blocks
    a, c = swap(a, c, 64, quarter < 2)
    b, d = swap(b, d, 64, quarter < 2)
    a, b = swap(a, b, 32, quarter % 2 == 0)
    c, d = swap(c, d, 32, quarter % 2 == 0)
    return a, b, c, d


def by_sequence(heads):
    first, second = swap_quarters(heads[:4]), swap_quarters(heads[4:])
    whole = [jnp.concatenate(two, axis=1).reshape(-1, 8, 256) for two in zip(first, second)]
    return jnp.stack(whole, axis=1).reshape(-1, 256)


def by_head(y):
    y = y.reshape(-1, 4, 8, 256)
    heads = []
    for half in range(2):
        blocks = [y[:, si, :, half * 128 : (half + 1) * 128].reshape(-1, 128) for si in range(4)]
        heads.extend(swap_quarters(blocks))
    return heads


def bias_kernel(duo_ref, w_ref, flags_ref, out_ref, rows_s):
    step = pl.program_id(0)

    @pl.when(step < 4)
    def _():
        x = duo_ref[...].reshape(16 * 128, 128).astype(jnp.float32)
        n = standardize(x).astype(jnp.bfloat16)
        heads = lax.dot_general(
            w_ref[...], n, (((0,), (1,)), ((), ())), preferred_element_type=jnp.float32
        )
        for i in range(16):
            rows_s[:, i, :] = heads[:, i * 128 : (i + 1) * 128] * LOG2E
        out_ref[...] = jnp.broadcast_to(rows_s[...].astype(jnp.bfloat16)[None], (2, 8, 16, 128))

    @pl.when(step == 4)
    def _():
        out_ref[...] = jnp.broadcast_to(flags_ref[...][None, None], (2, 8, 16, 128))


def bias_tile(duo, w, flags):
    return pl.pallas_call(
        bias_kernel,
        grid=(5,),
        in_specs=[
            pl.BlockSpec((16, 128, 128), lambda i: (jnp.minimum(i, 3), 0, 0)),
            pl.BlockSpec((128, 8), lambda i: (0, 0)),
            pl.BlockSpec((16, 128), lambda i: (0, 0)),
        ],
        out_specs=pl.BlockSpec((2, 8, 16, 128), lambda i: (0, 0, i, 0)),
        out_shape=jax.ShapeDtypeStruct((2, 8, 80, 128), jnp.bfloat16),
        scratch_shapes=[pltpu.VMEM((8, 16, 128), jnp.float32)],
        compiler_params=params(),
        cost_estimate=cost(20_000_000, 2_200_000),
        name="bias_tile",
    )(duo, w, flags)


def qkv_kernel(x_ref, wq_ref, wk_ref, wv_ref, early_ref, late_ref):
    groups = 16 // QKV_STEPS
    n = standardize(x_ref[...].reshape(groups * 128, 256).astype(jnp.float32))
    n = n.astype(jnp.bfloat16)
    for t, w in enumerate((wq_ref, wk_ref, wv_ref)):
        y = dot(n, w[...])
        if t == 0:
            y = y * (LOG2E / 32**0.5)
        for h, part in enumerate(by_head(y)):
            part = part.reshape(groups, 4, 8, 128).astype(jnp.bfloat16)
            for g in range(4):
                out_ref = early_ref if g < 2 else late_ref
                out_ref[h, t, g % 2] = part[:, g]


def qkv(x, wq, wk, wv):
    whole = pl.BlockSpec((256, 256), lambda i: (0, 0))
    return pl.pallas_call(
        qkv_kernel,
        grid=(QKV_STEPS,),
        in_specs=[
            pl.BlockSpec((16 // QKV_STEPS, 4, 4, 8, 256), lambda i: (i, 0, 0, 0, 0)),
            whole,
            whole,
            whole,
        ],
        out_specs=[pl.BlockSpec((8, 3, 2, 16 // QKV_STEPS, 8, 128), lambda i: (0, 0, 0, i, 0, 0))] * 2,
        out_shape=[jax.ShapeDtypeStruct((8, 3, 2, 16, 8, 128), jnp.bfloat16)] * 2,
        compiler_params=params(),
        cost_estimate=cost(800_000_000, 4_500_000),
        name="qkv",
    )(x, wq, wk, wv)


def natural(block):
    x = jnp.swapaxes(block.astype(jnp.float32), 0, 1)
    return x.reshape(x.shape[0] * 64, 128).astype(jnp.bfloat16)


def bias_tile_at(bias_ref, r, c):
    if bias_ref.shape[0] == 1:
        return bias_ref[0, 0, c, :64, :]
    return bias_ref[lax.rem(r, 8), lax.div(r, 8), c, :64, :]


def attend(
    block, blocks, q_ref, k_ref, v_ref, bias_ref, present, out_ref, q_s, k_s, v_s, which=0
):
    lane = iota((1, 128), 1) // 32
    wide_lane = (iota((1, 256), 1) // 32) % 4
    q_s[...] = natural(q_ref[:, 0, which])
    k_s[...] = natural(k_ref[:, 0, which])
    v_s[:, :128] = natural(v_ref[:, 0, which])

    @pl.when(pl.program_id(0) == 0)
    def _():
        v_s[:, 128:] = jnp.ones((1024, 128), jnp.bfloat16)

    tiles = block // 64

    def step(at, carry):
        rows = pl.ds(pl.multiple_of(at * block, block), block)
        q = q_s[rows, :]
        bias = jnp.concatenate(
            [
                jnp.concatenate([bias_tile_at(bias_ref, at * tiles + t, c) for c in range(8)], 1)
                for t in range(tiles)
            ],
            0,
        ).astype(jnp.float32)
        ones = [jnp.where(lane == si, q, jnp.zeros_like(q)) for si in range(4)]

        def probs(score, si):
            score = jnp.where(present[si : si + 1] > 0, score + bias, MASKED)
            top = jnp.max(score, axis=1, keepdims=True)
            return jnp.exp2(score - top).astype(jnp.bfloat16)

        if block > 64:
            parts = [dot(probs(dot(ones[si], k_s[...], NT), si), v_s[...]) for si in range(4)]
        else:
            scores = dot(jnp.concatenate(ones, 0), k_s[...], NT)
            parts = [probs(scores[si * block : (si + 1) * block], si) for si in range(4)]
            parts = dot(jnp.concatenate(parts, 0), v_s[...])
            parts = [parts[si * block : (si + 1) * block] for si in range(4)]
        total = parts[0]
        for si in range(1, 4):
            total = jnp.where(wide_lane == si, parts[si], total)
        result = total[:, :128] / total[:, 128:]
        eighth = block // 8
        out_ref[pl.ds(pl.multiple_of(at * eighth, eighth), eighth), 0, which] = result.reshape(
            eighth, 8, 128
        ).astype(jnp.bfloat16)
        return carry

    if blocks == 1:
        step(0, 0)
    else:
        lax.fori_loop(0, blocks, step, 0, unroll=UNROLL)


def first_kernel(
    at_ref, q_ref, k_ref, v_ref, bias_ref, flags_ref, out_ref, slab_ref, slab_bias_ref, mask_ref, *scratch
):
    @pl.when(pl.program_id(0) == 0)
    def _():
        both = flags_ref[...].astype(jnp.float32)
        flags = jnp.where(at_ref[1] // 8 == 0, both[..., :8, :], both[..., 8:, :])
        flags = jnp.swapaxes(flags, 0, 1)
        own = iota((16, 128), 1) == (at_ref[1] % 8) * 16 + iota((16, 128), 0)
        mask = dot(own.astype(jnp.bfloat16), flags.reshape(1024, 128).astype(jnp.bfloat16), NT)
        for g in range(4):
            mask_ref[g] = mask[g * 4 : g * 4 + 4]
        slab = at_ref[0]
        slab_bias_ref[0, 0] = bias_ref[lax.rem(slab, 8), lax.div(slab, 8), :, :64]

    present = mask_ref[pl.program_id(0)]
    attend(BLOCK, 1024 // BLOCK, q_ref, k_ref, v_ref, bias_ref, present, out_ref, *scratch)
    slab_ref[:, 0, 0] = out_ref[pl.ds(pl.multiple_of(at_ref[0] * 8, 8), 8), 0, 0]


def slab_kernel(at_ref, q_ref, k_ref, v_ref, bias_ref, mask_ref, _, out_ref, *scratch):
    for which in range(2):
        own = scratch[which * 3 : which * 3 + 3]
        attend(64, 1, q_ref, k_ref, v_ref, bias_ref, mask_ref[which], out_ref, *own, which)


def later_kernel(q_ref, k_ref, v_ref, bias_ref, mask_ref, *rest):
    attend(BLOCK, 1024 // BLOCK, q_ref, k_ref, v_ref, bias_ref, mask_ref[0], *rest[-4:])


def attention_scratch(rows):
    return [
        pltpu.VMEM((rows, 128), jnp.bfloat16),
        pltpu.VMEM((1024, 128), jnp.bfloat16),
        pltpu.VMEM((1024, 256), jnp.bfloat16),
    ]


RETURNED = jax.ShapeDtypeStruct((128, 1, 6, 8, 128), jnp.bfloat16)
SLAB_WEIGHTED = jax.ShapeDtypeStruct((8, 1, 4, 8, 128), jnp.bfloat16)


def first_attention(at, received, bias):
    part = lambda t: pl.BlockSpec((8, 1, 1, 16, 8, 128), lambda g, s: (0, t, g, 0, 0, 0))
    return pl.pallas_call(
        first_kernel,
        grid_spec=pltpu.PrefetchScalarGridSpec(
            num_scalar_prefetch=1,
            grid=(2,),
            in_specs=[
                part(0),
                part(1),
                part(2),
                pl.BlockSpec((8, 2, 8, 80, 128), lambda g, s: (0, 0, 0, 0, 0)),
                pl.BlockSpec((8, 2, 8, 16, 128), lambda g, s: (0, 0, 0, 4, 0)),
            ],
            out_specs=[
                pl.BlockSpec((128, 1, 1, 8, 128), lambda g, s: (0, 0, g, 0, 0)),
                pl.BlockSpec((8, 1, 1, 8, 128), lambda g, s: (0, 0, g, 0, 0)),
                pl.BlockSpec((1, 1, 8, 64, 128), lambda g, s: (0, 0, 0, 0, 0)),
                pl.BlockSpec((4, 4, 1024), lambda g, s: (0, 0, 0)),
            ],
            scratch_shapes=attention_scratch(1024),
        ),
        out_shape=[
            RETURNED,
            SLAB_WEIGHTED,
            jax.ShapeDtypeStruct((1, 1, 8, 64, 128), jnp.bfloat16),
            jax.ShapeDtypeStruct((4, 4, 1024), jnp.float32),
        ],
        compiler_params=params(),
        cost_estimate=cost(16_000_000_000, 4_000_000, 2 << 22),
        name="first_attention",
    )(at, received, received, received, bias, bias)


def slab_attention(at, received, bias, mask, onto):
    part = lambda t: pl.BlockSpec((8, 1, 2, 16, 8, 128), lambda g, s: (0, t, 0, 0, 0, 0))
    return pl.pallas_call(
        slab_kernel,
        grid_spec=pltpu.PrefetchScalarGridSpec(
            num_scalar_prefetch=1,
            grid=(1,),
            in_specs=[
                pl.BlockSpec((8, 1, 2, 1, 8, 128), lambda g, s: (0, 0, 0, s[0], 0, 0)),
                part(1),
                part(2),
                pl.BlockSpec((1, 1, 8, 64, 128), lambda g, s: (0, 0, 0, 0, 0)),
                pl.BlockSpec((2, 4, 1024), lambda g, s: (1, 0, 0)),
                pl.BlockSpec(memory_space=pl.ANY),
            ],
            out_specs=pl.BlockSpec((8, 1, 2, 8, 128), lambda g, s: (0, 0, 1, 0, 0)),
            scratch_shapes=attention_scratch(64) * 2,
        ),
        out_shape=SLAB_WEIGHTED,
        input_output_aliases={6: 0},
        compiler_params=params(),
        cost_estimate=cost(1_000_000_000, 2_000_000, 1 << 19),
        name="slab_attention",
    )(at, received, received, received, bias, mask, onto)


def later_attention(received, bias, mask, onto):
    part = lambda t: pl.BlockSpec((8, 1, 1, 16, 8, 128), lambda g: (0, t, g, 0, 0, 0))
    return pl.pallas_call(
        later_kernel,
        grid=(2,),
        in_specs=[
            part(0),
            part(1),
            part(2),
            pl.BlockSpec((8, 2, 8, 80, 128), lambda g: (0, 0, 0, 0, 0)),
            pl.BlockSpec((1, 4, 1024), lambda g: (g + 2, 0, 0)),
            pl.BlockSpec(memory_space=pl.ANY),
        ],
        out_specs=pl.BlockSpec((128, 1, 1, 8, 128), lambda g: (0, 0, g + 2, 0, 0)),
        out_shape=RETURNED,
        scratch_shapes=attention_scratch(1024),
        input_output_aliases={5: 0},
        compiler_params=params(),
        cost_estimate=cost(16_000_000_000, 4_000_000, 2 << 22),
        name="later_attention",
    )(received, received, received, bias, mask, onto)


def gates(x, w):
    return jax.nn.sigmoid(dot(standardize(x).astype(jnp.bfloat16), w))


def prepare_kernel(at_ref, x_ref, slab_ref, gate_ref, gates_ref, slab_gates_ref):
    x = x_ref[...].reshape(2048, 256).astype(jnp.float32)
    gates_ref[...] = gates(x, gate_ref[...]).astype(jnp.bfloat16)
    slab_gates_ref[...] = gates(slab_ref[0].reshape(128, 256).astype(jnp.float32), gate_ref[...])


def prepare(at, x, sequences, w_gate):
    whole = lambda *shape: pl.BlockSpec(shape, lambda i, s: (0,) * len(shape))
    return pl.pallas_call(
        prepare_kernel,
        grid_spec=pltpu.PrefetchScalarGridSpec(
            num_scalar_prefetch=1,
            grid=(1,),
            in_specs=[
                whole(256, 8, 256),
                pl.BlockSpec((1, 4, 4, 8, 256), lambda i, s: (s[0], 0, 0, 0, 0)),
                whole(256, 256),
            ],
            out_specs=[whole(2048, 256), whole(128, 256)],
        ),
        out_shape=[
            jax.ShapeDtypeStruct((2048, 256), jnp.bfloat16),
            jax.ShapeDtypeStruct((128, 256), jnp.float32),
        ],
        compiler_params=params(),
        cost_estimate=cost(300_000_000, 3_000_000),
        name="prepare",
    )(at, x, sequences, w_gate)


def gated_update(x, gate, heads, w_out):
    gated = (gate * by_sequence(heads)).astype(jnp.bfloat16)
    return (x + dot(gated, w_out)).astype(jnp.bfloat16).astype(jnp.float32)


def left_kernel(
    at_ref, x_ref, weighted_ref, flags_ref, gate_ref, out_w_ref, factor_ref, _, out_ref
):
    x = x_ref[0].reshape(128, 256).astype(jnp.float32)
    heads = [weighted_ref[h, 0].astype(jnp.float32).reshape(32, 128) for h in range(8)]
    fresh = gated_update(x, gate_ref[...], heads, out_w_ref[...])
    left = factor(standardize(fresh).astype(jnp.bfloat16), factor_ref[...], 1)
    left = left * flags_ref[...]
    for half in range(2):
        part = left[:, half * 128 : (half + 1) * 128].reshape(1, 2, 1, 8, 128)
        part = jnp.broadcast_to(part, (8, 2, 8, 8, 128)).reshape(128, 8, 128)
        out_ref[:, 0, half] = part.astype(jnp.bfloat16)


def left_factor(at, x, weighted, flags, gate, w_out, w_first, onto):
    whole = lambda *shape: pl.BlockSpec(shape, lambda i, s: (0,) * len(shape))
    return pl.pallas_call(
        left_kernel,
        grid_spec=pltpu.PrefetchScalarGridSpec(
            num_scalar_prefetch=1,
            grid=(1,),
            in_specs=[
                pl.BlockSpec((1, 4, 4, 8, 256), lambda i, s: (s[0], 0, 0, 0, 0)),
                whole(8, 1, 4, 8, 128),
                whole(16, 1),
                whole(128, 256),
                whole(256, 256),
                whole(256, 32),
                pl.BlockSpec(memory_space=pl.ANY),
            ],
            out_specs=pl.BlockSpec((128, 1, 2, 8, 128), lambda i, s: (0, 0, 2, 0, 0)),
        ),
        out_shape=RETURNED,
        input_output_aliases={7: 0},
        compiler_params=params(),
        cost_estimate=cost(100_000_000, 3_500_000),
        name="left_factor",
    )(at, x, weighted, flags, gate, w_out, w_first, onto)


def fresh_kernel(
    x_ref, weighted_ref, flags_ref, gate_ref, out_w_ref, factor_ref, fresh_ref, right_ref
):
    x = x_ref[...].reshape(2048, 256).astype(jnp.float32)
    heads = [weighted_ref[:, h, 0].astype(jnp.float32).reshape(512, 128) for h in range(8)]
    fresh = gated_update(x, gate_ref[...].astype(jnp.float32), heads, out_w_ref[...])
    fresh_ref[...] = fresh.reshape(256, 8, 256).astype(jnp.bfloat16)
    right = factor(standardize(fresh).astype(jnp.bfloat16), factor_ref[...], 32)
    right_ref[...] = (right * flags_ref[...]).astype(jnp.bfloat16)


def renew(x, returned, flags, gate, w_out, w_second):
    whole = lambda *shape: pl.BlockSpec(shape, lambda i: (0,) * len(shape))
    return pl.pallas_call(
        fresh_kernel,
        grid=(1,),
        in_specs=[
            whole(256, 8, 256),
            pl.BlockSpec((16, 8, 1, 4, 8, 128), lambda i: (0, 0, 0, 0, 0, 0)),
            whole(256, 1),
            whole(2048, 256),
            whole(256, 256),
            whole(256, 32),
        ],
        out_specs=[whole(256, 8, 256), whole(256, 256)],
        out_shape=[
            jax.ShapeDtypeStruct((256, 8, 256), jnp.bfloat16),
            jax.ShapeDtypeStruct((256, 256), jnp.bfloat16),
        ],
        compiler_params=params(36),
        cost_estimate=cost(1_500_000_000, 5_000_000),
        name="renew",
    )(x, returned, flags, gate, w_out, w_second)


def pair_kernel(at_ref, mine_ref, other_ref, right_ref, product_ref, pair_ref, outer_s, pair_s):
    own_first = lax.rem(at_ref[1], 2) == 0
    mine, other = mine_ref[...].astype(jnp.float32), other_ref[...].astype(jnp.float32)
    halves = (jnp.where(own_first, mine, other), jnp.where(own_first, other, mine))
    right = right_ref[...].astype(jnp.float32).reshape(16, 2, 8, 256)
    right = jnp.concatenate([right[:, half].reshape(128, 256) for half in range(2)], axis=0)
    right = right.astype(jnp.bfloat16)
    for c in range(8):
        left = jnp.concatenate(
            [
                jnp.concatenate([part[:, c, q].reshape(128, 128) for q in range(2)], axis=1)
                for part in halves
            ],
            axis=0,
        ).astype(jnp.bfloat16)
        outer_s[:, c] = (dot(left, right, TN) * (1.0 / 256)).reshape(32, 8, 256)
    for half in range(2):
        quads = [[] for _ in range(4)]
        for quad in range(8):
            parts = [
                outer_s[quad * 4 + u, :, :, half * 128 : (half + 1) * 128].reshape(64, 128)
                for u in range(4)
            ]
            for j, part in enumerate(swap_quarters(parts)):
                quads[j].append(part.astype(jnp.bfloat16))
        for j in range(4):
            pair_s[:, half * 4 + j, :] = dot(jnp.concatenate(quads[j], axis=1), product_ref[...])
    pair_ref[...] = pair_s[...].astype(jnp.bfloat16)


def pair_mean(at, mine, other, right, w_product):
    whole = lambda *shape: pl.BlockSpec(shape, lambda i, s: (0,) * len(shape))
    return pl.pallas_call(
        pair_kernel,
        grid_spec=pltpu.PrefetchScalarGridSpec(
            num_scalar_prefetch=1,
            grid=(1,),
            in_specs=[
                whole(16, 8, 2, 8, 128),
                whole(16, 8, 2, 8, 128),
                whole(256, 256),
                whole(1024, 128),
            ],
            out_specs=whole(64, 8, 128),
            scratch_shapes=[
                pltpu.VMEM((32, 8, 8, 256), jnp.float32),
                pltpu.VMEM((64, 8, 128), jnp.float32),
            ],
        ),
        out_shape=jax.ShapeDtypeStruct((64, 8, 128), jnp.bfloat16),
        compiler_params=params(36),
        cost_estimate=cost(500_000_000, 2_000_000),
        name="pair_mean",
    )(at, mine, other, right, w_product)


def exchange(x, axes):
    return lax.all_to_all(x, axes, split_axis=0, concat_axis=0, tiled=True)


def per_device(
    alignment_tensor,
    amino_exists_flags,
    chain_exists_flags,
    chosen_slab_number,
    duo_tensor,
    duo_offset_matrix,
    asking_matrix,
    lookup_matrix,
    content_matrix,
    sigmoid_matrix,
    final_projection_matrix,
    first_factor_matrix,
    second_factor_matrix,
    product_to_duo_matrix,
):
    row = lax.axis_index(ROW)
    at = jnp.concatenate([chosen_slab_number, jnp.reshape(row, (1,)).astype(jnp.int32)])
    sequences = exchange(alignment_tensor, ROW).reshape(16, 4, 4, 8, 256)

    flags = jnp.transpose(amino_exists_flags.reshape(2, 128, 8), (0, 2, 1))
    flags = flags.reshape(16, 128).astype(jnp.bfloat16)
    tile = bias_tile(duo_tensor, duo_offset_matrix, flags)
    sequences, tile = lax.optimization_barrier((sequences, tile))
    tile = exchange(tile.reshape(16, 80, 128), ("xl",) + COL)
    early, late = qkv(sequences, asking_matrix, lookup_matrix, content_matrix)
    early, late, tile = lax.optimization_barrier((early, late, tile))
    bias = lax.all_gather(tile.reshape(2, 8, 80, 128), ("y", "core"), axis=0, tiled=False)
    early = exchange(early, COL)
    late, early = lax.optimization_barrier((late, early))
    late = exchange(late, COL)

    chains = chain_exists_flags.astype(jnp.float32)[:, None]
    own_chains = lax.dynamic_slice_in_dim(chains, row * 16, 16, 0)
    gate, slab_gate = prepare(at, alignment_tensor, sequences, sigmoid_matrix)

    early, gate, slab_gate = lax.optimization_barrier((early, gate, slab_gate))
    returned, slab_weighted, slab_bias, mask = first_attention(at, early, bias)
    slab_weighted = slab_attention(at, late, slab_bias, mask, slab_weighted)
    slab_weighted = exchange(slab_weighted, COL)
    returned = later_attention(late, bias, mask, returned)
    slab_weighted, returned = lax.optimization_barrier((slab_weighted, returned))
    returned = left_factor(
        at,
        sequences,
        slab_weighted,
        own_chains,
        slab_gate,
        final_projection_matrix,
        first_factor_matrix,
        returned,
    )
    returned = exchange(returned, BOTH).reshape(16, 8, 6, 8, 128)
    mine = returned[:, :, 4:]
    other = lax.ppermute(mine, "core", [(0, 1), (1, 0)])
    fresh, right = renew(
        alignment_tensor,
        returned.reshape(16, 8, 1, 6, 8, 128),
        chains,
        gate,
        final_projection_matrix,
        second_factor_matrix,
    )
    return fresh, pair_mean(at, mine, other, right, product_to_duo_matrix)


def solution(mesh):
    mesh = jax.sharding.Mesh(mesh.devices.reshape(2, 4, 2, 2, 4), BOTH)
    placed = (
        P(None, BOTH, None),
        P(None, BOTH),
        P(),
        P(),
        P(ROW, COL, None),
    ) + (P(),) * 9
    return jax.shard_map(
        per_device,
        mesh=mesh,
        in_specs=placed,
        out_specs=(P(None, BOTH, None), P(None, BOTH, None)),
        check_vma=False,
    )
```

```python
import functools

import jax
import jax.numpy as jnp
from jax import lax
from jax.experimental import pallas as pl
from jax.experimental.pallas import tpu as pltpu
from jax.sharding import PartitionSpec as P

LOG2E = 1.4426950408889634
MASKED = -1e9 * LOG2E
ROW = ("xl", "y", "core")
COL = ("xh", "z")
BOTH = ROW + COL
BLOCK, UNROLL = 256, 4
QKV_STEPS = 2
NT = (((1,), (1,)), ((), ()))
TN = (((0,), (0,)), ((), ()))


def dot(a, b, dims=None):
    if dims is None:
        return jnp.dot(a, b, preferred_element_type=jnp.float32)
    return lax.dot_general(a, b, dims, preferred_element_type=jnp.float32)


def params(mib=60):
    return pltpu.CompilerParams(vmem_limit_bytes=mib << 20)


def cost(flops, moved, exps=0):
    return pl.CostEstimate(flops=flops, bytes_accessed=moved, transcendentals=exps)


def standardize(x):
    mean = jnp.mean(x, axis=-1, keepdims=True)
    centred = x - mean
    var = jnp.mean(centred * centred, axis=-1, keepdims=True)
    return centred * lax.rsqrt(var + 1e-05)


def iota(shape, dim):
    return lax.broadcasted_iota(jnp.int32, shape, dim)


def factor(normed, w, across):
    row, col = iota((32, 256), 0), iota((32, 256), 1)
    channel, residue = (col % 32, col // 32) if across == 32 else (col // 8, col % 8)
    wide = dot(w, (row == channel).astype(jnp.bfloat16)).astype(jnp.bfloat16)
    y = dot(normed, wide).reshape(-1, 8, 256)
    own = iota((1, 8, 256), 1) == residue[:1].reshape(1, 1, 256)
    return jnp.sum(jnp.where(own, y, 0.0), axis=1)


def swap_quarters(blocks):
    quarter = iota((1, 128), 1) // 32

    def swap(a, b, shift, keep):
        return (
            jnp.where(keep, a, pltpu.roll(b, shift, 1)),
            jnp.where(keep, pltpu.roll(a, 128 - shift, 1), b),
        )

    a, b, c, d = blocks
    a, c = swap(a, c, 64, quarter < 2)
    b, d = swap(b, d, 64, quarter < 2)
    a, b = swap(a, b, 32, quarter % 2 == 0)
    c, d = swap(c, d, 32, quarter % 2 == 0)
    return a, b, c, d


def by_sequence(heads):
    first, second = swap_quarters(heads[:4]), swap_quarters(heads[4:])
    whole = [jnp.concatenate(two, axis=1).reshape(-1, 8, 256) for two in zip(first, second)]
    return jnp.stack(whole, axis=1).reshape(-1, 256)


def by_head(y):
    y = y.reshape(-1, 4, 8, 256)
    heads = []
    for half in range(2):
        blocks = [y[:, si, :, half * 128 : (half + 1) * 128].reshape(-1, 128) for si in range(4)]
        heads.extend(swap_quarters(blocks))
    return heads


def bias_kernel(duo_ref, w_ref, flags_ref, out_ref, rows_s):
    step = pl.program_id(0)

    @pl.when(step < 4)
    def _():
        x = duo_ref[...].reshape(16 * 128, 128).astype(jnp.float32)
        n = standardize(x).astype(jnp.bfloat16)
        heads = lax.dot_general(
            w_ref[...], n, (((0,), (1,)), ((), ())), preferred_element_type=jnp.float32
        )
        for i in range(16):
            rows_s[:, i, :] = heads[:, i * 128 : (i + 1) * 128] * LOG2E
        out_ref[...] = jnp.broadcast_to(rows_s[...].astype(jnp.bfloat16)[None], (2, 8, 16, 128))

    @pl.when(step == 4)
    def _():
        out_ref[...] = jnp.broadcast_to(flags_ref[...][None, None], (2, 8, 16, 128))


def bias_tile(duo, w, flags):
    return pl.pallas_call(
        bias_kernel,
        grid=(5,),
        in_specs=[
            pl.BlockSpec((16, 128, 128), lambda i: (jnp.minimum(i, 3), 0, 0)),
            pl.BlockSpec((128, 8), lambda i: (0, 0)),
            pl.BlockSpec((16, 128), lambda i: (0, 0)),
        ],
        out_specs=pl.BlockSpec((2, 8, 16, 128), lambda i: (0, 0, i, 0)),
        out_shape=jax.ShapeDtypeStruct((2, 8, 80, 128), jnp.bfloat16),
        scratch_shapes=[pltpu.VMEM((8, 16, 128), jnp.float32)],
        compiler_params=params(),
        cost_estimate=cost(20_000_000, 2_200_000),
        name="bias_tile",
    )(duo, w, flags)


def qkv_kernel(x_ref, wq_ref, wk_ref, wv_ref, early_ref, late_ref):
    groups = 16 // QKV_STEPS
    n = standardize(x_ref[...].reshape(groups * 128, 256).astype(jnp.float32))
    n = n.astype(jnp.bfloat16)
    for t, w in enumerate((wq_ref, wk_ref, wv_ref)):
        y = dot(n, w[...])
        if t == 0:
            y = y * (LOG2E / 32**0.5)
        for h, part in enumerate(by_head(y)):
            part = part.reshape(groups, 4, 8, 128).astype(jnp.bfloat16)
            for g in range(4):
                out_ref = early_ref if g < 2 else late_ref
                out_ref[h, t, g % 2] = part[:, g]


def qkv(x, wq, wk, wv):
    whole = pl.BlockSpec((256, 256), lambda i: (0, 0))
    return pl.pallas_call(
        qkv_kernel,
        grid=(QKV_STEPS,),
        in_specs=[
            pl.BlockSpec((16 // QKV_STEPS, 4, 4, 8, 256), lambda i: (i, 0, 0, 0, 0)),
            whole,
            whole,
            whole,
        ],
        out_specs=[pl.BlockSpec((8, 3, 2, 16 // QKV_STEPS, 8, 128), lambda i: (0, 0, 0, i, 0, 0))] * 2,
        out_shape=[jax.ShapeDtypeStruct((8, 3, 2, 16, 8, 128), jnp.bfloat16)] * 2,
        compiler_params=params(),
        cost_estimate=cost(800_000_000, 4_500_000),
        name="qkv",
    )(x, wq, wk, wv)


def natural(block):
    x = jnp.swapaxes(block.astype(jnp.float32), 0, 1)
    return x.reshape(x.shape[0] * 64, 128).astype(jnp.bfloat16)


def bias_tile_at(bias_ref, r, c):
    if bias_ref.shape[0] == 1:
        return bias_ref[0, 0, c, :64, :]
    return bias_ref[lax.rem(r, 8), lax.div(r, 8), c, :64, :]


def attend(
    block, blocks, q_ref, k_ref, v_ref, bias_ref, present, out_ref, q_s, k_s, v_s, which=0
):
    lane = iota((1, 128), 1) // 32
    wide_lane = (iota((1, 256), 1) // 32) % 4
    q_s[...] = natural(q_ref[:, 0, which])
    k_s[...] = natural(k_ref[:, 0, which])
    v_s[:, :128] = natural(v_ref[:, 0, which])

    @pl.when(pl.program_id(0) == 0)
    def _():
        v_s[:, 128:] = jnp.ones((1024, 128), jnp.bfloat16)

    tiles = block // 64

    def step(at, carry):
        rows = pl.ds(pl.multiple_of(at * block, block), block)
        q = q_s[rows, :]
        bias = jnp.concatenate(
            [
                jnp.concatenate([bias_tile_at(bias_ref, at * tiles + t, c) for c in range(8)], 1)
                for t in range(tiles)
            ],
            0,
        ).astype(jnp.float32)
        ones = [jnp.where(lane == si, q, jnp.zeros_like(q)) for si in range(4)]

        def probs(score, si):
            score = jnp.where(present[si : si + 1] > 0, score + bias, MASKED)
            top = jnp.max(score, axis=1, keepdims=True)
            return jnp.exp2(score - top).astype(jnp.bfloat16)

        if block > 64:
            parts = [dot(probs(dot(ones[si], k_s[...], NT), si), v_s[...]) for si in range(4)]
        else:
            scores = dot(jnp.concatenate(ones, 0), k_s[...], NT)
            parts = [probs(scores[si * block : (si + 1) * block], si) for si in range(4)]
            parts = dot(jnp.concatenate(parts, 0), v_s[...])
            parts = [parts[si * block : (si + 1) * block] for si in range(4)]
        total = parts[0]
        for si in range(1, 4):
            total = jnp.where(wide_lane == si, parts[si], total)
        result = total[:, :128] / total[:, 128:]
        eighth = block // 8
        out_ref[pl.ds(pl.multiple_of(at * eighth, eighth), eighth), 0, which] = result.reshape(
            eighth, 8, 128
        ).astype(jnp.bfloat16)
        return carry

    if blocks == 1:
        step(0, 0)
    else:
        lax.fori_loop(0, blocks, step, 0, unroll=UNROLL)


def first_kernel(
    at_ref, q_ref, k_ref, v_ref, bias_ref, flags_ref, out_ref, slab_ref, slab_bias_ref, mask_ref, *scratch
):
    @pl.when(pl.program_id(0) == 0)
    def _():
        both = flags_ref[...].astype(jnp.float32)
        flags = jnp.where(at_ref[1] // 8 == 0, both[..., :8, :], both[..., 8:, :])
        flags = jnp.swapaxes(flags, 0, 1)
        own = iota((16, 128), 1) == (at_ref[1] % 8) * 16 + iota((16, 128), 0)
        mask = dot(own.astype(jnp.bfloat16), flags.reshape(1024, 128).astype(jnp.bfloat16), NT)
        for g in range(4):
            mask_ref[g] = mask[g * 4 : g * 4 + 4]
        slab = at_ref[0]
        slab_bias_ref[0, 0] = bias_ref[lax.rem(slab, 8), lax.div(slab, 8), :, :64]

    present = mask_ref[pl.program_id(0)]
    attend(BLOCK, 1024 // BLOCK, q_ref, k_ref, v_ref, bias_ref, present, out_ref, *scratch)
    slab_ref[:, 0, 0] = out_ref[pl.ds(pl.multiple_of(at_ref[0] * 8, 8), 8), 0, 0]


def slab_kernel(at_ref, q_ref, k_ref, v_ref, bias_ref, mask_ref, _, out_ref, *scratch):
    for which in range(2):
        own = scratch[which * 3 : which * 3 + 3]
        attend(64, 1, q_ref, k_ref, v_ref, bias_ref, mask_ref[which], out_ref, *own, which)


def later_kernel(q_ref, k_ref, v_ref, bias_ref, mask_ref, *rest):
    attend(BLOCK, 1024 // BLOCK, q_ref, k_ref, v_ref, bias_ref, mask_ref[0], *rest[-4:])


def attention_scratch(rows):
    return [
        pltpu.VMEM((rows, 128), jnp.bfloat16),
        pltpu.VMEM((1024, 128), jnp.bfloat16),
        pltpu.VMEM((1024, 256), jnp.bfloat16),
    ]


RETURNED = jax.ShapeDtypeStruct((128, 1, 6, 8, 128), jnp.bfloat16)
SLAB_WEIGHTED = jax.ShapeDtypeStruct((8, 1, 4, 8, 128), jnp.bfloat16)


def first_attention(at, received, bias):
    part = lambda t: pl.BlockSpec((8, 1, 1, 16, 8, 128), lambda g, s: (0, t, g, 0, 0, 0))
    return pl.pallas_call(
        first_kernel,
        grid_spec=pltpu.PrefetchScalarGridSpec(
            num_scalar_prefetch=1,
            grid=(2,),
            in_specs=[
                part(0),
                part(1),
                part(2),
                pl.BlockSpec((8, 2, 8, 80, 128), lambda g, s: (0, 0, 0, 0, 0)),
                pl.BlockSpec((8, 2, 8, 16, 128), lambda g, s: (0, 0, 0, 4, 0)),
            ],
            out_specs=[
                pl.BlockSpec((128, 1, 1, 8, 128), lambda g, s: (0, 0, g, 0, 0)),
                pl.BlockSpec((8, 1, 1, 8, 128), lambda g, s: (0, 0, g, 0, 0)),
                pl.BlockSpec((1, 1, 8, 64, 128), lambda g, s: (0, 0, 0, 0, 0)),
                pl.BlockSpec((4, 4, 1024), lambda g, s: (0, 0, 0)),
            ],
            scratch_shapes=attention_scratch(1024),
        ),
        out_shape=[
            RETURNED,
            SLAB_WEIGHTED,
            jax.ShapeDtypeStruct((1, 1, 8, 64, 128), jnp.bfloat16),
            jax.ShapeDtypeStruct((4, 4, 1024), jnp.float32),
        ],
        compiler_params=params(),
        cost_estimate=cost(16_000_000_000, 4_000_000, 2 << 22),
        name="first_attention",
    )(at, received, received, received, bias, bias)


def slab_attention(at, received, bias, mask, onto):
    part = lambda t: pl.BlockSpec((8, 1, 2, 16, 8, 128), lambda g, s: (0, t, 0, 0, 0, 0))
    return pl.pallas_call(
        slab_kernel,
        grid_spec=pltpu.PrefetchScalarGridSpec(
            num_scalar_prefetch=1,
            grid=(1,),
            in_specs=[
                pl.BlockSpec((8, 1, 2, 1, 8, 128), lambda g, s: (0, 0, 0, s[0], 0, 0)),
                part(1),
                part(2),
                pl.BlockSpec((1, 1, 8, 64, 128), lambda g, s: (0, 0, 0, 0, 0)),
                pl.BlockSpec((2, 4, 1024), lambda g, s: (1, 0, 0)),
                pl.BlockSpec(memory_space=pl.ANY),
            ],
            out_specs=pl.BlockSpec((8, 1, 2, 8, 128), lambda g, s: (0, 0, 1, 0, 0)),
            scratch_shapes=attention_scratch(64) * 2,
        ),
        out_shape=SLAB_WEIGHTED,
        input_output_aliases={6: 0},
        compiler_params=params(),
        cost_estimate=cost(1_000_000_000, 2_000_000, 1 << 19),
        name="slab_attention",
    )(at, received, received, received, bias, mask, onto)


def later_attention(received, bias, mask, onto):
    part = lambda t: pl.BlockSpec((8, 1, 1, 16, 8, 128), lambda g: (0, t, g, 0, 0, 0))
    return pl.pallas_call(
        later_kernel,
        grid=(2,),
        in_specs=[
            part(0),
            part(1),
            part(2),
            pl.BlockSpec((8, 2, 8, 80, 128), lambda g: (0, 0, 0, 0, 0)),
            pl.BlockSpec((1, 4, 1024), lambda g: (g + 2, 0, 0)),
            pl.BlockSpec(memory_space=pl.ANY),
        ],
        out_specs=pl.BlockSpec((128, 1, 1, 8, 128), lambda g: (0, 0, g + 2, 0, 0)),
        out_shape=RETURNED,
        scratch_shapes=attention_scratch(1024),
        input_output_aliases={5: 0},
        compiler_params=params(),
        cost_estimate=cost(16_000_000_000, 4_000_000, 2 << 22),
        name="later_attention",
    )(received, received, received, bias, mask, onto)


def gates(x, w):
    return jax.nn.sigmoid(dot(standardize(x).astype(jnp.bfloat16), w))


def prepare_kernel(at_ref, x_ref, slab_ref, gate_ref, gates_ref, slab_gates_ref):
    x = x_ref[...].reshape(2048, 256).astype(jnp.float32)
    gates_ref[0] = gates(x, gate_ref[...]).astype(jnp.bfloat16)
    gates_ref[1] = x_ref[...].reshape(2048, 256)
    slab_gates_ref[...] = gates(slab_ref[0].reshape(128, 256).astype(jnp.float32), gate_ref[...])


def prepare(at, x, sequences, w_gate):
    whole = lambda *shape: pl.BlockSpec(shape, lambda i, s: (0,) * len(shape))
    return pl.pallas_call(
        prepare_kernel,
        grid_spec=pltpu.PrefetchScalarGridSpec(
            num_scalar_prefetch=1,
            grid=(1,),
            in_specs=[
                whole(256, 8, 256),
                pl.BlockSpec((1, 4, 4, 8, 256), lambda i, s: (s[0], 0, 0, 0, 0)),
                whole(256, 256),
            ],
            out_specs=[whole(2, 2048, 256), whole(128, 256)],
        ),
        out_shape=[
            jax.ShapeDtypeStruct((2, 2048, 256), jnp.bfloat16),
            jax.ShapeDtypeStruct((128, 256), jnp.float32),
        ],
        compiler_params=params(),
        cost_estimate=cost(300_000_000, 3_000_000),
        name="prepare",
    )(at, x, sequences, w_gate)


def gated_update(x, gate, heads, w_out):
    gated = (gate * by_sequence(heads)).astype(jnp.bfloat16)
    return (x + dot(gated, w_out)).astype(jnp.bfloat16).astype(jnp.float32)


def left_kernel(
    at_ref, x_ref, weighted_ref, flags_ref, gate_ref, out_w_ref, factor_ref, _, out_ref
):
    x = x_ref[0].reshape(128, 256).astype(jnp.float32)
    heads = [weighted_ref[h, 0].astype(jnp.float32).reshape(32, 128) for h in range(8)]
    fresh = gated_update(x, gate_ref[...], heads, out_w_ref[...])
    left = factor(standardize(fresh).astype(jnp.bfloat16), factor_ref[...], 1)
    left = left * flags_ref[...]
    for half in range(2):
        part = left[:, half * 128 : (half + 1) * 128].reshape(1, 2, 1, 8, 128)
        part = jnp.broadcast_to(part, (8, 2, 8, 8, 128)).reshape(128, 8, 128)
        out_ref[:, 0, half] = part.astype(jnp.bfloat16)


def left_factor(at, x, weighted, flags, gate, w_out, w_first, onto):
    whole = lambda *shape: pl.BlockSpec(shape, lambda i, s: (0,) * len(shape))
    return pl.pallas_call(
        left_kernel,
        grid_spec=pltpu.PrefetchScalarGridSpec(
            num_scalar_prefetch=1,
            grid=(1,),
            in_specs=[
                pl.BlockSpec((1, 4, 4, 8, 256), lambda i, s: (s[0], 0, 0, 0, 0)),
                whole(8, 1, 4, 8, 128),
                whole(16, 1),
                whole(128, 256),
                whole(256, 256),
                whole(256, 32),
                pl.BlockSpec(memory_space=pl.ANY),
            ],
            out_specs=pl.BlockSpec((128, 1, 2, 8, 128), lambda i, s: (0, 0, 2, 0, 0)),
        ),
        out_shape=RETURNED,
        input_output_aliases={7: 0},
        compiler_params=params(),
        cost_estimate=cost(100_000_000, 3_500_000),
        name="left_factor",
    )(at, x, weighted, flags, gate, w_out, w_first, onto)


def fresh_kernel(own_ref, weighted_ref, flags_ref, out_w_ref, factor_ref, fresh_ref, right_ref):
    x = own_ref[1].astype(jnp.float32)
    heads = [weighted_ref[:, h, 0].astype(jnp.float32).reshape(512, 128) for h in range(8)]
    fresh = gated_update(x, own_ref[0].astype(jnp.float32), heads, out_w_ref[...])
    fresh_ref[...] = fresh.reshape(256, 8, 256).astype(jnp.bfloat16)
    right = factor(standardize(fresh).astype(jnp.bfloat16), factor_ref[...], 32)
    right_ref[...] = (right * flags_ref[...]).astype(jnp.bfloat16)


def renew(own, returned, flags, w_out, w_second):
    whole = lambda *shape: pl.BlockSpec(shape, lambda i: (0,) * len(shape))
    return pl.pallas_call(
        fresh_kernel,
        grid=(1,),
        in_specs=[
            whole(2, 2048, 256),
            pl.BlockSpec((16, 8, 1, 4, 8, 128), lambda i: (0, 0, 0, 0, 0, 0)),
            whole(256, 1),
            whole(256, 256),
            whole(256, 32),
        ],
        out_specs=[whole(256, 8, 256), whole(256, 256)],
        out_shape=[
            jax.ShapeDtypeStruct((256, 8, 256), jnp.bfloat16),
            jax.ShapeDtypeStruct((256, 256), jnp.bfloat16),
        ],
        compiler_params=params(36),
        cost_estimate=cost(1_500_000_000, 5_000_000),
        name="renew",
    )(own, returned, flags, w_out, w_second)


def pair_kernel(at_ref, mine_ref, other_ref, right_ref, product_ref, pair_ref, outer_s, pair_s):
    own_first = lax.rem(at_ref[1], 2) == 0
    mine, other = mine_ref[...].astype(jnp.float32), other_ref[...].astype(jnp.float32)
    halves = (jnp.where(own_first, mine, other), jnp.where(own_first, other, mine))
    right = right_ref[...].astype(jnp.float32).reshape(16, 2, 8, 256)
    right = jnp.concatenate([right[:, half].reshape(128, 256) for half in range(2)], axis=0)
    right = right.astype(jnp.bfloat16)
    for c in range(8):
        left = jnp.concatenate(
            [
                jnp.concatenate([part[:, c, q].reshape(128, 128) for q in range(2)], axis=1)
                for part in halves
            ],
            axis=0,
        ).astype(jnp.bfloat16)
        outer_s[:, c] = (dot(left, right, TN) * (1.0 / 256)).reshape(32, 8, 256)
    for half in range(2):
        quads = [[] for _ in range(4)]
        for quad in range(8):
            parts = [
                outer_s[quad * 4 + u, :, :, half * 128 : (half + 1) * 128].reshape(64, 128)
                for u in range(4)
            ]
            for j, part in enumerate(swap_quarters(parts)):
                quads[j].append(part.astype(jnp.bfloat16))
        for j in range(4):
            pair_s[:, half * 4 + j, :] = dot(jnp.concatenate(quads[j], axis=1), product_ref[...])
    pair_ref[...] = pair_s[...].astype(jnp.bfloat16)


def pair_mean(at, mine, other, right, w_product):
    whole = lambda *shape: pl.BlockSpec(shape, lambda i, s: (0,) * len(shape))
    return pl.pallas_call(
        pair_kernel,
        grid_spec=pltpu.PrefetchScalarGridSpec(
            num_scalar_prefetch=1,
            grid=(1,),
            in_specs=[
                whole(16, 8, 2, 8, 128),
                whole(16, 8, 2, 8, 128),
                whole(256, 256),
                whole(1024, 128),
            ],
            out_specs=whole(64, 8, 128),
            scratch_shapes=[
                pltpu.VMEM((32, 8, 8, 256), jnp.float32),
                pltpu.VMEM((64, 8, 128), jnp.float32),
            ],
        ),
        out_shape=jax.ShapeDtypeStruct((64, 8, 128), jnp.bfloat16),
        compiler_params=params(36),
        cost_estimate=cost(500_000_000, 2_000_000),
        name="pair_mean",
    )(at, mine, other, right, w_product)


def exchange(x, axes):
    return lax.all_to_all(x, axes, split_axis=0, concat_axis=0, tiled=True)


def per_device(
    alignment_tensor,
    amino_exists_flags,
    chain_exists_flags,
    chosen_slab_number,
    duo_tensor,
    duo_offset_matrix,
    asking_matrix,
    lookup_matrix,
    content_matrix,
    sigmoid_matrix,
    final_projection_matrix,
    first_factor_matrix,
    second_factor_matrix,
    product_to_duo_matrix,
):
    row = lax.axis_index(ROW)
    at = jnp.concatenate([chosen_slab_number, jnp.reshape(row, (1,)).astype(jnp.int32)])
    sequences = exchange(alignment_tensor, ROW).reshape(16, 4, 4, 8, 256)

    flags = jnp.transpose(amino_exists_flags.reshape(2, 128, 8), (0, 2, 1))
    flags = flags.reshape(16, 128).astype(jnp.bfloat16)
    tile = bias_tile(duo_tensor, duo_offset_matrix, flags)
    sequences, tile = lax.optimization_barrier((sequences, tile))
    tile = exchange(tile.reshape(16, 80, 128), ("xl",) + COL)
    early, late = qkv(sequences, asking_matrix, lookup_matrix, content_matrix)
    early, late, tile = lax.optimization_barrier((early, late, tile))
    bias = lax.all_gather(tile.reshape(2, 8, 80, 128), ("y", "core"), axis=0, tiled=False)
    early = exchange(early, COL)
    late, early = lax.optimization_barrier((late, early))
    late = exchange(late, COL)

    chains = chain_exists_flags.astype(jnp.float32)[:, None]
    own_chains = lax.dynamic_slice_in_dim(chains, row * 16, 16, 0)
    own, slab_gate = prepare(at, alignment_tensor, sequences, sigmoid_matrix)

    early, own, slab_gate = lax.optimization_barrier((early, own, slab_gate))
    returned, slab_weighted, slab_bias, mask = first_attention(at, early, bias)
    slab_weighted = slab_attention(at, late, slab_bias, mask, slab_weighted)
    slab_weighted = exchange(slab_weighted, COL)
    returned = later_attention(late, bias, mask, returned)
    slab_weighted, returned = lax.optimization_barrier((slab_weighted, returned))
    returned = left_factor(
        at,
        sequences,
        slab_weighted,
        own_chains,
        slab_gate,
        final_projection_matrix,
        first_factor_matrix,
        returned,
    )
    returned = exchange(returned, BOTH).reshape(16, 8, 6, 8, 128)
    mine = returned[:, :, 4:]
    other = lax.ppermute(mine, "core", [(0, 1), (1, 0)])
    fresh, right = renew(
        own,
        returned.reshape(16, 8, 1, 6, 8, 128),
        chains,
        final_projection_matrix,
        second_factor_matrix,
    )
    return fresh, pair_mean(at, mine, other, right, product_to_duo_matrix)


def solution(mesh):
    mesh = jax.sharding.Mesh(mesh.devices.reshape(2, 4, 2, 2, 4), BOTH)
    placed = (
        P(None, BOTH, None),
        P(None, BOTH),
        P(),
        P(),
        P(ROW, COL, None),
    ) + (P(),) * 9
    return jax.shard_map(
        per_device,
        mesh=mesh,
        in_specs=placed,
        out_specs=(P(None, BOTH, None), P(None, BOTH, None)),
        check_vma=False,
    )
```
